256 devices in a mesh: band: 4 (over x), ga: 64 (over z, y, core).
Axes of the slice: x: 4, y: 4, z: 8, core: 2. Of those that a mesh axis runs over, the one named last changes fastest.
Arguments:
- psi_valence: bfloat16 [2, 2, 128, 18432], P(None, None, 'ga'), may hold values from -6 to 6
- psi_conduction: bfloat16 [2, 128, 128, 18432], P(None, 'band', 'ga'), may hold values from -6 to 6
- val_energy: float32 [2], replicated, may hold values from -2 to -0.5
- cond_energy: float32 [128], P('band'), may hold values from 0.3 to 10
- miller: int32 [3, 40960], P(None, 'ga'), may hold values from -96 to 95, as said below
- pair_list: int32 [2, 32], P(None, 'band'), may hold values from 0 to 127, as said below
Outputs:
- chi_slab: float32 [1024, 2, 40960], P('band', None, 'ga')
The draws below stay inside these ranges and needn't reach their ends.
Inputs may be any that keep to these rules, and one draw needn't show every extreme that they name: `miller`: rows 0, 1, 2 hold h in [-64, 64), k in [-48, 48), l in [-96, 96). The G vectors of columns j * 640 to (j + 1) * 640 - 1 are distinct and have (k mod 96) * 192 + (l mod 192) in [j * 288, (j + 1) * 288). `pair_list`: columns b * 8 to (b + 1) * 8 - 1 name distinct pairs, with row 0 a valence band below 2 and row 1 a conduction band in [b * 32, (b + 1) * 32); each such block holds the pair of the highest valence band, number 1, with conduction band (b + 1) * 32 - 1.
All inputs are finite; a program needn't handle non-finite values.
Results may differ from the reference program's by a relative error of at most 0.0003.
Values sent between devices are 32-bit elements; how exact they have to be, the bound alone decides.
A program may use at most 128 MiB of HBM per device.

```python
import math
import jax
import jax.numpy as jnp
from jax import lax

NX = 128
NY = 96
NZ = 192
NV = 2
C_DEV = 32
G_DEV = 640
ROW_DEV = 16
P_DEV = 8
NC = 128
NG = 40960
SLAB = 1024
NPAIRS = 32


def draw_miller(key, part):
    key = jax.random.fold_in(key, 11)
    block_count = NG // G_DEV
    block_points = NX * NY * NZ // block_count

    def draw_block(sub_key):
        return jax.random.permutation(sub_key, block_points)[:G_DEV].astype(jnp.int32)
    chosen = jax.vmap(draw_block)(jax.random.split(key, block_count))
    offsets = (jnp.arange(block_count, dtype=jnp.int32) * block_points)[:, None]
    flat_ids = (chosen + offsets).reshape(-1)
    first_idx = flat_ids % NX
    pencil = flat_ids // NX
    second_idx = pencil // NZ
    third_idx = pencil % NZ
    h_index = jnp.where(first_idx >= NX // 2, first_idx - NX, first_idx)
    k_index = jnp.where(second_idx >= NY // 2, second_idx - NY, second_idx)
    l_index = jnp.where(third_idx >= NZ // 2, third_idx - NZ, third_idx)
    return jnp.stack([h_index, k_index, l_index]).astype(jnp.int32)


def draw_pair_list(key, part):
    key = jax.random.fold_in(key, 23)
    block_count = NPAIRS // P_DEV

    def draw_block(sub_key):
        others = jax.random.permutation(sub_key, NV * C_DEV - 1)[:P_DEV - 1].astype(jnp.int32)
        return jnp.concatenate([others, jnp.full((1,), NV * C_DEV - 1, jnp.int32)])
    chosen = jax.vmap(draw_block)(jax.random.split(key, block_count))
    valence_ids = chosen // C_DEV
    offsets = (jnp.arange(block_count, dtype=jnp.int32) * C_DEV)[:, None]
    cond_ids = chosen % C_DEV + offsets
    return jnp.stack([valence_ids.reshape(-1), cond_ids.reshape(-1)]).astype(jnp.int32)


def levels(rng, dims, cuts, low, high):
    loudness = 1.0
    for axis_at, shards_of in cuts:
        draws = jax.random.uniform(jax.random.fold_in(jax.random.fold_in(rng, 6), axis_at), (shards_of,), jnp.float32, low / len(cuts), high / len(cuts))
        loudness = loudness * jnp.repeat(jnp.exp(draws), dims[axis_at] // shards_of).reshape((-1,) + (1,) * (len(dims) - 1 - axis_at))
    return loudness


def bell_draw(own_key, shape, scale, bound, cuts=(), held_as=jnp.bfloat16):
    values = scale * jax.random.normal(own_key, shape, jnp.float32)
    if cuts:
        values = values * levels(own_key, shape, cuts, -0.22, 0.18)
    return jnp.clip(values, -bound, bound).astype(held_as)


def setup_inputs(seed: int = 0) -> dict:
    seeds = jax.random.split(jax.random.key(seed), 7)
    psi_valence = bell_draw(seeds[0], (2, NV, NX, NY * NZ), 1.0, 6.0, ((2, 64),))
    psi_conduction = bell_draw(seeds[1], (2, NC, NX, NY * NZ), 1.0, 6.0, ((1, 4), (2, 64)))
    val_energy = jnp.clip(jax.random.uniform(seeds[2], (NV,), jnp.float32, -2.0, -0.5), -2.0, -0.5)
    cond_energy = jnp.clip(jnp.exp(math.log(10.0) - 3.506558 * jax.random.uniform(seeds[3], (NC,), jnp.float32) ** levels(seeds[3], (NC,), ((0, 4),), -0.2, 0.2)), 0.3, 10.0)
    miller = draw_miller(jax.random.fold_in(seeds[6], 71), 0)
    pair_list = draw_pair_list(jax.random.fold_in(seeds[6], 71), 0)
    return {"psi_valence": psi_valence, "psi_conduction": psi_conduction, "val_energy": val_energy, "cond_energy": cond_energy, "miller": miller, "pair_list": pair_list}


def reference(psi_valence, psi_conduction, val_energy, cond_energy, miller, pair_list):
    flat_index = ((jnp.mod(miller[1], NY) * NZ + jnp.mod(miller[2], NZ)) * NX + jnp.mod(miller[0], NX)).astype(jnp.int32)

    def single_pair(pair_entry):
        val_real = psi_valence[0, pair_entry[0]].astype(jnp.float32)
        val_imag = psi_valence[1, pair_entry[0]].astype(jnp.float32)
        cond_real = psi_conduction[0, pair_entry[1]].astype(jnp.float32)
        cond_imag = psi_conduction[1, pair_entry[1]].astype(jnp.float32)
        dens_real = val_real * cond_real + val_imag * cond_imag
        dens_imag = val_real * cond_imag - val_imag * cond_real
        density = (dens_real + 1j * dens_imag).reshape(NX, NY, NZ)
        spectrum = jnp.fft.fftn(density) / math.sqrt(NX * NY * NZ)
        flat_spectrum = jnp.transpose(spectrum, (1, 2, 0)).reshape(-1)
        picked = flat_spectrum[flat_index]
        return jnp.stack([jnp.real(picked), jnp.imag(picked)])
    amps = lax.map(single_pair, pair_list.T)
    weight = 4.0 / ((val_energy[pair_list[0]] - cond_energy[pair_list[1]]) * math.sqrt(NPAIRS))
    row_ids = jnp.arange(SLAB, dtype=jnp.int32)
    slab_columns = (row_ids // ROW_DEV * G_DEV + row_ids % ROW_DEV).astype(jnp.int32)
    left_side = amps[:, :, slab_columns] * weight[:, None, None]
    chi_real = jnp.dot(left_side[:, 0].T, amps[:, 0], precision=lax.Precision.HIGHEST) + jnp.dot(left_side[:, 1].T, amps[:, 1], precision=lax.Precision.HIGHEST)
    chi_imag = jnp.dot(left_side[:, 1].T, amps[:, 0], precision=lax.Precision.HIGHEST) - jnp.dot(left_side[:, 0].T, amps[:, 1], precision=lax.Precision.HIGHEST)
    return jnp.stack([chi_real, chi_imag], axis=1)
```

```python
import math

import jax
import jax.numpy as jnp
import numpy as np
from jax import lax
from jax.experimental import pallas as pl
from jax.experimental.pallas import tpu as pltpu
from jax.sharding import PartitionSpec as P

NX = 128
NY = 96
NZ = 192
ROW_DEV = 16
PAIRS = 8
GA = 64
ZN, YN, CN, BN = 8, 4, 2, 4
HALF_Y = NY // 2
PENCILS = NY * NZ // GA
G_DEV = 640
TILES = G_DEV // 128
MESH = pl.DeviceIdType.MESH
F32 = jnp.float32
BF16 = jnp.bfloat16


def split_np(table):
    high = table.astype(np.float32).astype(jnp.bfloat16)
    low = (table - high.astype(np.float64)).astype(jnp.bfloat16)
    return high, low


def z_table():
    points = np.arange(NZ)
    angle = 2.0 * np.pi * ((points[:, None] * points[None, :]) % NZ) / NZ
    cosine, sine = np.cos(angle), np.sin(angle)
    table = np.zeros((2, 512, 512))
    for parity in range(2):
        first = 64 * parity
        table[parity, first : first + NZ, 0:NZ] = cosine
        table[parity, first : first + NZ, 256 : 256 + NZ] = -sine
        table[parity, 256 + first : 256 + first + NZ, 0:NZ] = sine
        table[parity, 256 + first : 256 + first + NZ, 256 : 256 + NZ] = cosine
    return table


def y_table():
    k = np.arange(NY)[:, None]
    table = np.zeros((2, NY, 2, 2, HALF_Y))
    for parity in range(2):
        y = 2 * np.arange(HALF_Y)[None, :] + parity
        angle = 2.0 * np.pi * ((k * y) % NY) / NY
        table[0, :, 0, parity] = np.cos(angle)
        table[0, :, 1, parity] = np.sin(angle)
        table[1, :, 0, parity] = -np.sin(angle)
        table[1, :, 1, parity] = np.cos(angle)
    return table.reshape(2 * NY, 4 * HALF_Y)


def x_table():
    angle = 2.0 * np.pi * np.arange(NX) / NX
    norm = 1.0 / math.sqrt(NX * NY * NZ)
    table = np.stack([np.cos(angle), np.sin(angle)]) * norm
    return np.repeat(table[:, None, :], 8, axis=1).astype(np.float32)


def split(value):
    high = value.astype(BF16)
    low = (value - high.astype(F32)).astype(BF16)
    return high, low


def dot(a, b):
    return jnp.dot(a, b, preferred_element_type=F32)


def dot3(a_high, a_low, b_high, b_low):
    return dot(a_high, b_high) + (dot(a_high, b_low) + dot(a_low, b_high))


def coordinates():
    band = lax.axis_index("band")
    ga = lax.axis_index("ga")
    return band, ga // 8, (ga // 2) % 4, ga % 2


def device(band, z, y, c):
    return (band, z * 8 + y * 2 + c)


def greet(partners):
    barrier = pltpu.get_barrier_semaphore()
    for partner in partners:
        pl.semaphore_signal(barrier, inc=1, device_id=partner, device_id_type=MESH)
    pl.semaphore_wait(barrier, len(partners))


def send(src, dst, send_sem, recv_sem, partner):
    copy = pltpu.make_async_remote_copy(
        src_ref=src, dst_ref=dst, send_sem=send_sem, recv_sem=recv_sem, device_id=partner, device_id_type=MESH
    )
    copy.start()
    return copy


def miller_kernel(mine_ref, out_ref, all_ref, send_sem, recv_sem):
    band, z, y, c = coordinates()
    z_partners = [device(band, (z + d) % ZN, y, c) for d in range(1, ZN)]
    y_partners = [device(band, z, (y + d) % YN, c) for d in range(1, YN)]
    core_partner = device(band, z, y, 1 - c)
    greet(z_partners + y_partners + [core_partner])
    all_ref[z, y, c] = mine_ref[...]
    copies = []
    for n, partner in enumerate(z_partners):
        block = all_ref.at[z, y, c]
        copies.append(send(block, block, send_sem.at[n], recv_sem.at[n], partner))
    for copy in copies:
        copy.wait()
    copies = []
    for n, partner in enumerate(y_partners):
        block = all_ref.at[:, y, c]
        copies.append(send(block, block, send_sem.at[7 + n], recv_sem.at[7 + n], partner))
    for copy in copies:
        copy.wait()
    block = all_ref.at[:, :, c]
    send(block, block, send_sem.at[10], recv_sem.at[10], core_partner).wait()
    out_ref[...] = all_ref[...]


def gather_miller(mine):
    shape = (ZN, YN, CN, 2, G_DEV)
    vmem = pl.BlockSpec(memory_space=pltpu.VMEM)
    return pl.pallas_call(
        miller_kernel,
        out_shape=jax.ShapeDtypeStruct(shape, jnp.int32),
        in_specs=[vmem],
        out_specs=vmem,
        scratch_shapes=[
            pltpu.VMEM(shape, jnp.int32),
            pltpu.SemaphoreType.DMA((11,)),
            pltpu.SemaphoreType.DMA((11,)),
        ],
        compiler_params=pltpu.CompilerParams(collective_id=0, has_side_effects=True),
        name="miller_gather",
    )(mine)


def density_step(y2, pair_ref, cond_start, pv_ref, pc_ref, dens):
    lanes = pl.ds(pl.multiple_of(y2 * 384, 384), 384)
    for p in range(PAIRS):
        v = pair_ref[0, p]
        q = pair_ref[1, p] - cond_start
        vr = pv_ref[0, v, :, lanes].astype(F32)
        vi = pv_ref[1, v, :, lanes].astype(F32)
        cr = pc_ref[0, q, :, lanes].astype(F32)
        ci = pc_ref[1, q, :, lanes].astype(F32)
        rows = slice(2 * p, 2 * p + 2)
        dens[y2, rows, 0:384] = vr * cr + vi * ci
        dens[y2, rows, 384:768] = vr * ci - vi * cr


def partial_kernel(
    pair_ref, val_ref, cond_ref, pv_ref, pc_ref, wzh_ref, wzl_ref, wyh_ref, wyl_ref, wx_ref, miller_ref, out_ref, dens, zed, spec
):
    band = lax.axis_index("band")
    ga = lax.axis_index("ga")
    cond_start = band * 32

    @pl.loop(0, HALF_Y)
    def _(y2):
        density_step(y2, pair_ref, cond_start, pv_ref, pc_ref, dens)

    @pl.loop(0, 6)
    def _(block):
        rows = pl.ds(pl.multiple_of(block * 128, 128), 128)
        for parity in range(2):
            first = 128 * parity
            span = pl.ds(block * 8, 8)
            both = jnp.concatenate([dens[span, :, first : first + 256], dens[span, :, 384 + first : 640 + first]], axis=2)
            high, low = split(both.reshape(128, 512))
            result = dot3(high, low, wzh_ref[parity], wzl_ref[parity])
            for tile in range(4):
                zed[parity, tile, rows, :] = result[:, 128 * tile : 128 * tile + 128]

    for p in range(PAIRS):
        for plane in range(2):
            row = 2 * p + plane
            halves = [
                jnp.concatenate(
                    [
                        zed[parity, 2 * part + tile, pl.ds(row, HALF_Y, stride=16), :]
                        for part in range(2)
                        for parity in range(2)
                    ],
                    axis=0,
                )
                for tile in range(2)
            ]
            high, low = split(jnp.concatenate(halves, axis=1))
            result = dot3(wyh_ref[...], wyl_ref[...], high, low)
            for part in range(2):
                for tile in range(2):
                    spec[tile, pl.ds(part * 16 + plane * 8 + p, NY, stride=32), :] = result[
                        part * NY : (part + 1) * NY, 128 * tile : 128 * tile + 128
                    ]

    pair_rows = lax.broadcasted_iota(jnp.int32, (8, 128), 0)
    gap = jnp.ones((8, 128), F32)
    for p in range(PAIRS):
        value = cond_ref[pair_ref[1, p] - cond_start] - val_ref[pair_ref[0, p]]
        gap = jnp.where(pair_rows == p, value, gap)
    scale = jnp.sqrt(4.0 / (gap * math.sqrt(32.0)))
    x0 = 2 * ga
    cos_tab = wx_ref[0]
    sin_tab = wx_ref[1]

    def take(table, index):
        return jnp.take_along_axis(table, index, axis=1)

    @pl.loop(0, ZN * YN)
    def _(m):
        zd = m // YN
        yd = m % YN
        base = pl.multiple_of(m * 96, 96)
        for cd in range(2):
            tiles = ((0, 0), (0, 1), (1, 0)) if cd == 0 else ((1, 0), (1, 1), (2, 0), (2, 1))
            for g in range(TILES):
                lanes = slice(128 * g, 128 * g + 128)
                line = jnp.broadcast_to(miller_ref[zd, yd, cd, 0:1, lanes], (8, 128)) + 288 * cd
                h = jnp.broadcast_to(miller_ref[zd, yd, cd, 1:2, lanes], (8, 128))
                k_low = 0 if cd == 0 else 1
                k_step = (line >= (k_low + 1) * NZ).astype(jnp.int32)
                l = line - k_low * NZ - k_step * NZ
                index = l & 127
                code = 2 * k_step + (l >> 7)
                got = []
                for group in range(4):
                    value = None
                    for k_row, tile in tiles:
                        source = spec[tile, pl.ds(pl.multiple_of(base + (32 * k_row + 8 * group), 8), 8), :]
                        taken = take(source, index)
                        if value is None:
                            value = taken
                        else:
                            value = jnp.where(code == 2 * (k_row - k_low) + tile, taken, value)
                    got.append(value)
                re0, re1, im0, im1 = got
                angle0 = (h * x0) & 127
                angle1 = (angle0 + h) & 127
                c0, s0 = take(cos_tab, angle0), take(sin_tab, angle0)
                c1, s1 = take(cos_tab, angle1), take(sin_tab, angle1)
                out_re = (c0 * re0 + s0 * im0) + (c1 * re1 + s1 * im1)
                out_im = (c0 * im0 - s0 * re0) + (c1 * im1 - s1 * re1)
                out_ref[cd, yd, zd, 0:8, lanes] = out_re * scale
                out_ref[cd, yd, zd, 8:16, lanes] = out_im * scale


def partial_sums(pair_list, val_energy, cond_energy, psi_valence, psi_conduction, miller_all):
    vmem = pl.BlockSpec(memory_space=pltpu.VMEM)
    smem = pl.BlockSpec(memory_space=pltpu.SMEM)
    wzh, wzl = split_np(z_table())
    wyh, wyl = split_np(y_table())
    tables = [jnp.asarray(t) for t in (wzh, wzl, wyh, wyl, x_table())]
    return pl.pallas_call(
        partial_kernel,
        out_shape=jax.ShapeDtypeStruct((CN, YN, ZN, 16, G_DEV), F32),
        in_specs=[smem] * 3 + [vmem] * 8,
        out_specs=vmem,
        scratch_shapes=[
            pltpu.VMEM((HALF_Y, 16, 768), F32),
            pltpu.VMEM((2, 4, 768, 128), F32),
            pltpu.VMEM((2, NY * 32, 128), F32),
        ],
        compiler_params=pltpu.CompilerParams(vmem_limit_bytes=56 * 1024 * 1024),
        name="partial_sums",
    )(pair_list, val_energy, cond_energy, psi_valence, psi_conduction, *tables, miller_all)


def sum_kernel(u_ref, amps_ref, rows_ref, from_core, relayed, near, far, total, by_z, amps, rows, send_sem, recv_sem):
    band, z, y, c = coordinates()
    z_partners = [device(band, (z + d) % ZN, y, c) for d in range(1, ZN)]
    core_partner = device(band, z, y, 1 - c)
    ahead = (y + 1 + 2 * c) % YN
    behind = (y + 3 - 2 * c) % YN
    across = (y + 2) % YN
    x_partners = [device((band + d) % BN, z, y, c) for d in range(1, BN)]
    to_ahead = device(band, z, ahead, c)
    to_behind = device(band, z, behind, c)
    to_across = device(band, z, across, c)
    y_partners = [to_ahead, to_behind, to_across]
    greet(z_partners + [core_partner] + y_partners + x_partners)

    core_copies = []
    order = [across, ahead, behind, y]
    for n, yd in enumerate(order):
        core_copies.append(send(u_ref.at[1 - c, yd], from_core.at[yd], send_sem.at[n], recv_sem.at[n], core_partner))

    core_copies[0].wait_recv()
    from_core[across] += u_ref[c, across]
    relay = send(from_core.at[across], relayed, send_sem.at[4], recv_sem.at[4], to_ahead)
    core_copies[1].wait_recv()
    from_core[behind] += u_ref[c, behind]
    back = send(from_core.at[behind], near, send_sem.at[5], recv_sem.at[5], to_behind)
    core_copies[2].wait_recv()
    from_core[ahead] += u_ref[c, ahead]
    relay.wait_recv()
    from_core[ahead] += relayed[...]
    forth = send(from_core.at[ahead], far, send_sem.at[6], recv_sem.at[6], to_ahead)
    core_copies[3].wait_recv()
    total[...] = from_core[y] + u_ref[c, y]
    back.wait_recv()
    total[...] += near[...]
    forth.wait_recv()
    total[...] += far[...]

    z_copies = []
    for n, partner in enumerate(z_partners):
        zd = (z + n + 1) % ZN
        z_copies.append(send(total.at[zd], by_z.at[n], send_sem.at[7 + n], recv_sem.at[7 + n], partner))
    result = total[z]
    for n, copy in enumerate(z_copies):
        copy.wait_recv()
        result = result + by_z[n]
    amps[band] = result
    x_copies = []
    for n, partner in enumerate(x_partners):
        x_copies.append(send(amps.at[band], amps.at[band], send_sem.at[14 + n], recv_sem.at[14 + n], partner))
    for copy in x_copies:
        copy.wait_recv()

    parts = [amps[b, :, 0:128] for b in range(BN)]
    for_real = [-part for part in parts]
    for_imag = [piece for part in parts for piece in (-part[8:16], part[0:8])]
    own = jnp.concatenate(for_real + for_imag, axis=0).T[0:ROW_DEV]
    z_home = 2 * band
    is_home = z // 2 == band

    @pl.when(is_home)
    def _():
        rows[z % 2, y, c] = own

    def row_copy(z2, n, partner):
        block = rows.at[z2, y, c]
        return pltpu.make_async_remote_copy(
            src_ref=block,
            dst_ref=block,
            send_sem=send_sem.at[17 + n],
            recv_sem=recv_sem.at[17 + z2],
            device_id=partner,
            device_id_type=MESH,
        )

    @pl.when(is_home)
    def _():
        for n, partner in enumerate(z_partners):
            row_copy(z % 2, n, partner).start()

    for z2 in range(2):

        @pl.when(z != z_home + z2)
        def _():
            row_copy(z2, 0, z_partners[0]).wait_recv()

    core_rows = rows.at[:, y, c]
    send(core_rows, core_rows, send_sem.at[24], recv_sem.at[19], core_partner).wait()
    y_copies = []
    for n, partner in enumerate(y_partners):
        block = rows.at[:, y]
        y_copies.append(send(block, block, send_sem.at[25 + n], recv_sem.at[20 + n], partner))
    amps_ref[...] = amps[...]
    for copy in y_copies:
        copy.wait()

    rows_ref[...] = rows[...]
    for copy in core_copies + [relay, back, forth] + z_copies + x_copies:
        copy.wait_send()

    @pl.when(is_home)
    def _():
        for n, partner in enumerate(z_partners):
            row_copy(z % 2, n, partner).wait_send()


def sum_up(partial):
    vmem = pl.BlockSpec(memory_space=pltpu.VMEM)
    block = (ZN, 16, G_DEV)
    return pl.pallas_call(
        sum_kernel,
        out_shape=(
            jax.ShapeDtypeStruct((BN, 16, G_DEV), F32),
            jax.ShapeDtypeStruct((2, YN, CN, ROW_DEV, 128), F32),
        ),
        in_specs=[vmem],
        out_specs=(vmem, vmem),
        scratch_shapes=[
            pltpu.VMEM((YN,) + block, F32),
            pltpu.VMEM(block, F32),
            pltpu.VMEM(block, F32),
            pltpu.VMEM(block, F32),
            pltpu.VMEM(block, F32),
            pltpu.VMEM((ZN - 1, 16, G_DEV), F32),
            pltpu.VMEM((BN, 16, G_DEV), F32),
            pltpu.VMEM((2, YN, CN, ROW_DEV, 128), F32),
            pltpu.SemaphoreType.DMA((28,)),
            pltpu.SemaphoreType.DMA((23,)),
        ],
        compiler_params=pltpu.CompilerParams(
            collective_id=1, has_side_effects=True, vmem_limit_bytes=32 * 1024 * 1024
        ),
        name="sum_up",
    )(partial)


def slab_kernel(rows_ref, amps_ref, out_ref):
    right_high, right_low = split(amps_ref[...].reshape(64, G_DEV))
    for part in range(2):
        left = rows_ref[...].reshape(256, 128)[:, 64 * part : 64 * part + 64]
        left_high, left_low = split(left)
        out_ref[:, part, :] = dot3(left_high, left_low, right_high, right_low)


def slab(rows, amps):
    vmem = pl.BlockSpec(memory_space=pltpu.VMEM)
    return pl.pallas_call(
        slab_kernel,
        out_shape=jax.ShapeDtypeStruct((256, 2, G_DEV), F32),
        in_specs=[vmem, vmem],
        out_specs=vmem,
        compiler_params=pltpu.CompilerParams(vmem_limit_bytes=32 * 1024 * 1024),
        name="slab",
    )(rows, amps)


def per_device(psi_valence, psi_conduction, val_energy, cond_energy, miller, pair_list):
    ga = lax.axis_index("ga")
    line = jnp.mod(miller[1], NY) * NZ + jnp.mod(miller[2], NZ) - ga * PENCILS
    mine = jnp.stack([line, jnp.mod(miller[0], NX)])
    miller_all = gather_miller(mine)
    partial = partial_sums(pair_list, val_energy, cond_energy, psi_valence, psi_conduction, miller_all)
    amps, rows = sum_up(partial)
    return slab(rows, amps)


def solution(mesh):
    return jax.shard_map(
        per_device,
        mesh=mesh,
        in_specs=(
            P(None, None, "ga", None),
            P(None, "band", "ga", None),
            P(),
            P("band"),
            P(None, "ga"),
            P(None, "band"),
        ),
        out_specs=P("band", None, "ga"),
        check_vma=False,
    )
```

```python
import math

import jax
import jax.numpy as jnp
import numpy as np
from jax import lax
from jax.experimental import pallas as pl
from jax.experimental.pallas import tpu as pltpu
from jax.sharding import PartitionSpec as P

NX = 128
NY = 96
NZ = 192
ROW_DEV = 16
PAIRS = 8
GA = 64
ZN, YN, CN, BN = 8, 4, 2, 4
HALF_Y = NY // 2
PENCILS = NY * NZ // GA
G_DEV = 640
TILES = G_DEV // 128
MESH = pl.DeviceIdType.MESH
F32 = jnp.float32
BF16 = jnp.bfloat16


def split_np(table):
    high = table.astype(np.float32).astype(jnp.bfloat16)
    low = (table - high.astype(np.float64)).astype(jnp.bfloat16)
    return high, low


def z_table():
    points = np.arange(NZ)
    angle = 2.0 * np.pi * ((points[:, None] * points[None, :]) % NZ) / NZ
    cosine, sine = np.cos(angle), np.sin(angle)
    table = np.zeros((2, 2, 256, 2, 2, 128))
    for parity in range(2):
        rows = slice(64 * parity, 64 * parity + NZ)
        for part_in in range(2):
            for part_out in range(2):
                values = cosine if part_in == part_out else (sine if part_in else -sine)
                for half in range(2):
                    table[parity, part_in, rows, part_out, half, 0:96] = values[:, 96 * half : 96 * half + 96]
    return table.reshape(2, 512, 512)


def y_table():
    k = np.arange(NY)[:, None]
    table = np.zeros((2, NY, 2, 2, HALF_Y))
    for parity in range(2):
        y = 2 * np.arange(HALF_Y)[None, :] + parity
        angle = 2.0 * np.pi * ((k * y) % NY) / NY
        table[0, :, 0, parity] = np.cos(angle)
        table[0, :, 1, parity] = np.sin(angle)
        table[1, :, 0, parity] = -np.sin(angle)
        table[1, :, 1, parity] = np.cos(angle)
    return table.reshape(2 * NY, 4 * HALF_Y)


def x_table():
    angle = 2.0 * np.pi * np.arange(NX) / NX
    norm = 1.0 / math.sqrt(NX * NY * NZ)
    return np.tile(np.stack([np.cos(angle), np.sin(angle)]) * norm, (4, 1)).astype(np.float32)


def split(value):
    high = value.astype(BF16)
    low = (value - high.astype(F32)).astype(BF16)
    return high, low


def dot(a, b):
    return jnp.dot(a, b, preferred_element_type=F32)


def dot3(a_high, a_low, b_high, b_low):
    return dot(a_high, b_high) + (dot(a_high, b_low) + dot(a_low, b_high))


def coordinates():
    band = lax.axis_index("band")
    ga = lax.axis_index("ga")
    return band, ga // 8, (ga // 2) % 4, ga % 2


def device(band, z, y, c):
    return (band, z * 8 + y * 2 + c)


def greet(partners):
    barrier = pltpu.get_barrier_semaphore()
    for partner in partners:
        pl.semaphore_signal(barrier, inc=1, device_id=partner, device_id_type=MESH)
    pl.semaphore_wait(barrier, len(partners))


def send(src, dst, send_sem, recv_sem, partner):
    copy = pltpu.make_async_remote_copy(
        src_ref=src, dst_ref=dst, send_sem=send_sem, recv_sem=recv_sem, device_id=partner, device_id_type=MESH
    )
    copy.start()
    return copy


def density_step(first, step, chosen, pv_ref, pc_ref, dens):
    lanes = pl.ds(pl.multiple_of(step * 384, 384), 384)
    y2 = first + step
    for p in range(PAIRS):
        v, q = chosen[p]
        vr = pv_ref[0, v, :, lanes].astype(F32)
        vi = pv_ref[1, v, :, lanes].astype(F32)
        cr = pc_ref[0, q, :, lanes].astype(F32)
        ci = pc_ref[1, q, :, lanes].astype(F32)
        rows = slice(2 * p, 2 * p + 2)
        dens[y2, rows, 0:384] = vr * cr + vi * ci
        dens[y2, rows, 384:768] = vr * ci - vi * cr


def transform_planes(
    chosen, pv_refs, pc_refs, wzh_ref, wzl_ref, wyh_ref, wyl_ref, dens, zed, spec, wait_psi, wait_tables, after_density
):
    for piece in range(PIECES):
        wait_psi(piece)

        @pl.loop(0, HALF_Y // PIECES // 2)
        def _(step):
            for u in range(2):
                density_step(piece * (HALF_Y // PIECES), step * 2 + u, chosen, pv_refs[piece], pc_refs[piece], dens)

    after_density()
    wait_tables()
    for parity in range(2):
        first = 128 * parity
        both = jnp.concatenate([dens[:, :, first : first + 256], dens[:, :, 384 + first : 640 + first]], axis=2)
        high, low = split(both.reshape(768, 512))
        result = dot3(high, low, wzh_ref[parity], wzl_ref[parity])
        for tile in range(4):
            zed[parity, tile] = result[:, 128 * tile : 128 * tile + 128]
    for p in range(PAIRS):
        for plane in range(2):
            row = 2 * p + plane
            halves = [
                jnp.concatenate(
                    [
                        zed[parity, 2 * part + tile, pl.ds(row, HALF_Y, stride=16), :]
                        for part in range(2)
                        for parity in range(2)
                    ],
                    axis=0,
                )
                for tile in range(2)
            ]
            high, low = split(jnp.concatenate(halves, axis=1))
            result = dot3(wyh_ref[...], wyl_ref[...], high, low)
            for part in range(2):
                for tile in range(2):
                    spec[tile, pl.ds(part * 16 + plane * 8 + p, NY, stride=32), :] = result[
                        part * NY : (part + 1) * NY, 128 * tile : 128 * tile + 128
                    ]


def take(table, index):
    return jnp.take_along_axis(table, index, axis=1)


def partial_block(m, cd, miller_of, table, plane_of_row, scale, spec, store):
    base = pl.multiple_of(m * 96, 96)
    for g in range(TILES):
        lanes = slice(128 * g, 128 * g + 128)
        line = jnp.broadcast_to(miller_of(0, lanes), (8, 128))
        h = jnp.broadcast_to(miller_of(1, lanes), (8, 128))
        second = line >= 96
        third = line >= 192
        index = line - jnp.where(third, 192, jnp.where(second, 96, 0))
        phases = take(table, (h * plane_of_row) & 127)
        c0, s0, c1, s1 = [jnp.broadcast_to(phases[i : i + 1], (8, 128)) for i in range(4)]
        got = []
        for group in range(4):
            values = []
            for tile in range(3):
                k_row, half = (3 * cd + tile) // 2, (3 * cd + tile) % 2
                rows = pl.ds(pl.multiple_of(base + (32 * k_row + 8 * group), 8), 8)
                values.append(take(spec[half, rows, :], index))
            got.append(jnp.where(third, values[2], jnp.where(second, values[1], values[0])))
        re0, re1, im0, im1 = got
        out_re = (c0 * re0 + s0 * im0) + (c1 * re1 + s1 * im1)
        out_im = (c0 * im0 - s0 * re0) + (c1 * im1 - s1 * re1)
        store(slice(0, 8), lanes, out_re * scale)
        store(slice(8, 16), lanes, out_im * scale)


LAGS = (0, 2), (2, 0), (2, 2), (3, 2)
PIECES = 3
CHUNKS = 4
SLOTS = ZN // CHUNKS
FIRST = 3
OWN = ZN - FIRST


def main_kernel(
    pair_ref,
    val_ref,
    cond_ref,
    pv_hbm,
    pc_hbm,
    wzh_hbm,
    wzl_hbm,
    wyh_hbm,
    wyl_hbm,
    wx_ref,
    miller_ref,
    amps_ref,
    rows_ref,
    pv_refs,
    pc_refs,
    wzh_ref,
    wzl_ref,
    wyh_ref,
    wyl_ref,
    dens,
    zed,
    spec,
    lines,
    sums,
    from_core,
    relayed,
    near,
    far,
    total,
    by_z,
    amps,
    rows,
    x_out,
    x_in,
    z_out,
    z_in,
    load_sem,
    send_sem,
    recv_sem,
):
    band, z, y, c = coordinates()
    psi_loads = []
    for piece in range(PIECES):
        lanes = pl.ds(piece * (NY * NZ // PIECES), NY * NZ // PIECES)
        for n, (src, dst) in enumerate(((pv_hbm, pv_refs[piece]), (pc_hbm, pc_refs[piece]))):
            copy = pltpu.make_async_copy(src.at[:, :, :, lanes], dst, load_sem.at[2 * piece + n])
            copy.start()
            psi_loads.append(copy)
    table_loads = []
    for n, (src, dst) in enumerate(
        ((wzh_hbm, wzh_ref), (wzl_hbm, wzl_ref), (wyh_hbm, wyh_ref), (wyl_hbm, wyl_ref))
    ):
        copy = pltpu.make_async_copy(src, dst, load_sem.at[2 * PIECES + n])
        copy.start()
        table_loads.append(copy)

    def wait_psi(piece):
        for copy in psi_loads[2 * piece : 2 * piece + 2]:
            copy.wait()

    def wait_tables():
        for copy in table_loads:
            copy.wait()

    z_partners = [device(band, (z + d) % ZN, y, c) for d in range(1, ZN)]
    x_partners = [device((band + d) % BN, z, y, c) for d in range(1, BN)]
    core_partner = device(band, z, y, 1 - c)
    plane_partners = [core_partner] + [
        device(band, z, (y + d) % YN, (c + e) % CN) for d in range(1, YN) for e in range(CN)
    ]
    ahead = (y + 1 + 2 * c) % YN
    behind = (y + 3 - 2 * c) % YN
    across = (y + 2) % YN
    to_ahead = device(band, z, ahead, c)
    to_behind = device(band, z, behind, c)

    k = miller_ref[1:2, :]
    l = miller_ref[2:3, :]
    lines[z, y, c, 0:1, :] = jnp.where(k < 0, k + NY, k) * NZ + jnp.where(l < 0, l + NZ, l) - (z * 8 + y * 2 + c) * PENCILS
    lines[z, y, c, 1:2, :] = miller_ref[0:1, :] & (NX - 1)
    greet(z_partners + x_partners + plane_partners)

    sent = []

    def start(slot, src, dst, partner):
        copy = send(src, dst, send_sem.at[slot], recv_sem.at[slot], partner)
        sent.append(copy)
        return copy

    mine = lines.at[z, y, c]
    line_copies = [start(n, mine, mine, partner) for n, partner in enumerate(z_partners)]

    def pass_lines_on():
        for copy in line_copies:
            copy.wait_recv()
        block = lines.at[:, y, c]
        for n, partner in enumerate(plane_partners):
            line_copies.append(start(7 + n, block, block, partner))

    chosen = [(pair_ref[0, p] & 1, pair_ref[1, p] & 31) for p in range(PAIRS)]
    pair_rows = lax.broadcasted_iota(jnp.int32, (8, 128), 0)
    gap = jnp.ones((8, 128), F32)
    for p, (v, q) in enumerate(chosen):
        gap = jnp.where(pair_rows == p, cond_ref[q] - val_ref[v], gap)
    scale = jnp.sqrt(4.0 / (gap * math.sqrt(32.0)))
    plane_of_row = 2 * (z * 8 + y * 2 + c) + ((pair_rows >> 1) & 1)
    table = wx_ref[...]

    transform_planes(
        chosen, pv_refs, pc_refs, wzh_ref, wzl_ref, wyh_ref, wyl_ref, dens, zed, spec, wait_psi, wait_tables, pass_lines_on
    )
    for copy in line_copies[7:]:
        copy.wait_recv()

    def add_up(yd, chunk):
        @pl.loop(0, SLOTS)
        def _(step):
            slot = chunk * SLOTS + step
            zd = (z + slot + FIRST) % ZN
            for cd in range(CN):

                def miller_of(kind, lanes):
                    return lines[zd, yd, cd, kind : kind + 1, lanes]

                def store(sublanes, lanes, value):
                    sums[cd, yd, slot, sublanes, lanes] = value

                partial_block(zd * YN + yd, cd, miller_of, table, plane_of_row, scale, spec, store)

    def part(ref, chunk, *index):
        return ref.at[(*index, pl.ds(chunk * SLOTS, SLOTS))]

    def exchange(chunk, n, yd):
        slot = 14 + 7 * chunk + n
        return start(slot, part(sums, chunk, 1 - c, yd), part(from_core, chunk, yd), core_partner)

    def join(copy, chunk, yd):
        copy.wait_recv()
        part(from_core, chunk, yd)[...] += part(sums, chunk, c, yd)[...]

    flows = [{} for _ in range(CHUNKS)]

    def send_relay(chunk):
        join(flows[chunk]["core", 0], chunk, across)
        flows[chunk]["relay"] = start(
            14 + 7 * chunk + 4, part(from_core, chunk, across), part(relayed, chunk), to_ahead
        )

    def send_back(chunk):
        join(flows[chunk]["core", 1], chunk, behind)
        flows[chunk]["back"] = start(14 + 7 * chunk + 5, part(from_core, chunk, behind), part(near, chunk), to_behind)

    def send_forth(chunk):
        join(flows[chunk]["core", 2], chunk, ahead)
        flows[chunk]["relay"].wait_recv()
        part(from_core, chunk, ahead)[...] += part(relayed, chunk)[...]
        flows[chunk]["forth"] = start(14 + 7 * chunk + 6, part(from_core, chunk, ahead), part(far, chunk), to_ahead)

    along_z = 14 + 7 * CHUNKS
    z_copies = []

    def send_z(chunk):
        flows[chunk]["core", 3].wait_recv()
        part(total, chunk)[...] = part(from_core, chunk, y)[...] + part(sums, chunk, c, y)[...]
        flows[chunk]["back"].wait_recv()
        flows[chunk]["forth"].wait_recv()
        part(total, chunk)[...] += part(near, chunk)[...] + part(far, chunk)[...]
        for slot in range(chunk * SLOTS, chunk * SLOTS + SLOTS):
            if slot != OWN:
                partner = device(band, (z + slot + FIRST) % ZN, y, c)
                z_copies.append((slot, start(along_z + slot, total.at[slot], by_z.at[slot], partner)))

    order = [across, ahead, behind, y]
    plan = {}
    for chunk in range(CHUNKS):
        for (n, lag), action in zip(LAGS, (send_relay, send_back, send_forth, send_z)):
            plan.setdefault(n * CHUNKS + chunk + lag, []).append((action, chunk))
    for step in range(max(plan) + 1):
        if step < 4 * CHUNKS:
            n, chunk = divmod(step, CHUNKS)
            add_up(order[n], chunk)
            flows[chunk]["core", n] = exchange(chunk, n, order[n])
        for action, chunk in plan.get(step, []):
            action(chunk)

    x_rows = along_z + 8
    z_rows = x_rows + 3
    plane_rows = z_rows + 7
    along_x = plane_rows + 7

    def own_rows(to_band, z2):
        return total[(2 * to_band + z2 - z - FIRST + 2 * ZN) % ZN, :, 0:128]

    x_row_copies = []
    for n, partner in enumerate(x_partners):
        for z2 in range(2):
            x_out[n, z2] = own_rows((band + n + 1) % BN, z2)
        x_row_copies.append(start(x_rows + n, x_out.at[n], x_in.at[band], partner))
    for z2 in range(2):
        x_in[band, z2] = own_rows(band, z2)
    for copy in x_row_copies:
        copy.wait_recv()
    for z2 in range(2):
        parts = [x_in[b, z2] for b in range(BN)]
        for_real = [-piece for piece in parts]
        for_imag = [piece for both in parts for piece in (-both[8:16], both[0:8])]
        z_out[z2] = jnp.concatenate(for_real + for_imag, axis=0).T[0:ROW_DEV]
    z_row_copies = [start(z_rows + n, z_out, z_in.at[n], partner) for n, partner in enumerate(z_partners)]

    result = total[OWN]
    for slot, copy in z_copies:
        copy.wait_recv()
        result = result + by_z[slot]
    amps[band] = result
    amp_copies = [
        start(along_x + n, amps.at[band], amps.at[band], partner) for n, partner in enumerate(x_partners)
    ]
    own = z_out[...]
    for n, copy in enumerate(z_row_copies):
        copy.wait_recv()
        own = own + z_in[n]
    for z2 in range(2):
        rows[z2, y, c] = own[z2]
    block = rows.at[:, y, c]
    row_copies = [start(plane_rows + n, block, block, partner) for n, partner in enumerate(plane_partners)]
    for copy in amp_copies:
        copy.wait_recv()
    amps_ref[...] = amps[...]
    for copy in row_copies:
        copy.wait_recv()
    rows_ref[...] = rows[...]
    for copy in sent:
        copy.wait_send()


def amplitudes(pair_list, val_energy, cond_energy, psi_valence, psi_conduction, miller):
    vmem = pl.BlockSpec(memory_space=pltpu.VMEM)
    smem = pl.BlockSpec(memory_space=pltpu.SMEM)
    wzh, wzl = split_np(z_table())
    wyh, wyl = split_np(y_table())
    tables = [jnp.asarray(t) for t in (wzh, wzl, wyh, wyl, x_table())]
    block = (ZN, 16, G_DEV)
    return pl.pallas_call(
        main_kernel,
        out_shape=(
            jax.ShapeDtypeStruct((BN, 16, G_DEV), F32),
            jax.ShapeDtypeStruct((2, YN, CN, ROW_DEV, 128), F32),
        ),
        in_specs=[smem] * 3 + [pl.BlockSpec(memory_space=pl.ANY)] * 6 + [vmem] * 2,
        out_specs=(vmem, vmem),
        scratch_shapes=[
            [pltpu.VMEM((2, 2, 2, NY * NZ // PIECES), BF16)] * PIECES,
            [pltpu.VMEM((2, 32, 2, NY * NZ // PIECES), BF16)] * PIECES,
            pltpu.VMEM(wzh.shape, BF16),
            pltpu.VMEM(wzl.shape, BF16),
            pltpu.VMEM(wyh.shape, BF16),
            pltpu.VMEM(wyl.shape, BF16),
            pltpu.VMEM((HALF_Y, 16, 768), F32),
            pltpu.VMEM((2, 4, 768, 128), F32),
            pltpu.VMEM((2, NY * 32, 128), F32),
            pltpu.VMEM((ZN, YN, CN, 2, G_DEV), jnp.int32),
            pltpu.VMEM((CN, YN) + block, F32),
            pltpu.VMEM((YN,) + block, F32),
            pltpu.VMEM(block, F32),
            pltpu.VMEM(block, F32),
            pltpu.VMEM(block, F32),
            pltpu.VMEM(block, F32),
            pltpu.VMEM(block, F32),
            pltpu.VMEM((BN, 16, G_DEV), F32),
            pltpu.VMEM((2, YN, CN, ROW_DEV, 128), F32),
            pltpu.VMEM((BN - 1, 2, 16, 128), F32),
            pltpu.VMEM((BN, 2, 16, 128), F32),
            pltpu.VMEM((2, ROW_DEV, 128), F32),
            pltpu.VMEM((ZN - 1, 2, ROW_DEV, 128), F32),
            pltpu.SemaphoreType.DMA((2 * PIECES + 4,)),
            pltpu.SemaphoreType.DMA((14 + 7 * CHUNKS + 28,)),
            pltpu.SemaphoreType.DMA((14 + 7 * CHUNKS + 28,)),
        ],
        compiler_params=pltpu.CompilerParams(
            collective_id=0, has_side_effects=True, vmem_limit_bytes=56 * 1024 * 1024
        ),
        name="amplitudes",
    )(pair_list, val_energy, cond_energy, psi_valence, psi_conduction, *tables, miller)


def slab_kernel(rows_ref, amps_ref, out_ref):
    right_high, right_low = split(amps_ref[...].reshape(64, G_DEV))
    for part in range(2):
        left = rows_ref[...].reshape(256, 128)[:, 64 * part : 64 * part + 64]
        left_high, left_low = split(left)
        out_ref[:, part, :] = dot3(left_high, left_low, right_high, right_low)


def slab(rows, amps):
    vmem = pl.BlockSpec(memory_space=pltpu.VMEM)
    return pl.pallas_call(
        slab_kernel,
        out_shape=jax.ShapeDtypeStruct((256, 2, G_DEV), F32),
        in_specs=[vmem, vmem],
        out_specs=vmem,
        compiler_params=pltpu.CompilerParams(vmem_limit_bytes=60 * 1024 * 1024),
        name="slab",
    )(rows, amps)


def per_device(psi_valence, psi_conduction, val_energy, cond_energy, miller, pair_list):
    amps, rows = amplitudes(pair_list, val_energy, cond_energy, psi_valence, psi_conduction, miller)
    return slab(rows, amps)


def solution(mesh):
    return jax.shard_map(
        per_device,
        mesh=mesh,
        in_specs=(
            P(None, None, "ga", None),
            P(None, "band", "ga", None),
            P(),
            P("band"),
            P(None, "ga"),
            P(None, "band"),
        ),
        out_specs=P("band", None, "ga"),
        check_vma=False,
    )
```

```python
import math

import jax
import jax.numpy as jnp
import numpy as np
from jax import lax
from jax.experimental import pallas as pl
from jax.experimental.pallas import tpu as pltpu
from jax.sharding import PartitionSpec as P

NX = 128
NY = 96
NZ = 192
ROW_DEV = 16
PAIRS = 8
GA = 64
ZN, YN, CN, BN = 8, 4, 2, 4
HALF_Y = NY // 2
PENCILS = NY * NZ // GA
G_DEV = 640
TILES = G_DEV // 128
MESH = pl.DeviceIdType.MESH
F32 = jnp.float32
BF16 = jnp.bfloat16


def split_np(table):
    high = table.astype(np.float32).astype(jnp.bfloat16)
    low = (table - high.astype(np.float64)).astype(jnp.bfloat16)
    return high, low


def z_table():
    points = np.arange(NZ)
    angle = 2.0 * np.pi * ((points[:, None] * points[None, :]) % NZ) / NZ
    cosine, sine = np.cos(angle), np.sin(angle)
    table = np.zeros((2, 2, 256, 2, 2, 128))
    for parity in range(2):
        rows = slice(64 * parity, 64 * parity + NZ)
        for part_in in range(2):
            for part_out in range(2):
                values = cosine if part_in == part_out else (sine if part_in else -sine)
                for half in range(2):
                    table[parity, part_in, rows, part_out, half, 0:96] = values[:, 96 * half : 96 * half + 96]
    return table.reshape(2, 512, 512)


def y_table():
    k = np.arange(NY)[:, None]
    table = np.zeros((2, NY, 2, 2, HALF_Y))
    for parity in range(2):
        y = 2 * np.arange(HALF_Y)[None, :] + parity
        angle = 2.0 * np.pi * ((k * y) % NY) / NY
        table[0, :, 0, parity] = np.cos(angle)
        table[0, :, 1, parity] = np.sin(angle)
        table[1, :, 0, parity] = -np.sin(angle)
        table[1, :, 1, parity] = np.cos(angle)
    return table.reshape(2 * NY, 4 * HALF_Y)


def x_table():
    angle = 2.0 * np.pi * np.arange(NX) / NX
    norm = 1.0 / math.sqrt(NX * NY * NZ)
    return np.tile(np.stack([np.cos(angle), np.sin(angle)]) * norm, (4, 1)).astype(np.float32)


def split(value):
    high = value.astype(BF16)
    low = (value - high.astype(F32)).astype(BF16)
    return high, low


def dot(a, b):
    return jnp.dot(a, b, preferred_element_type=F32)


def dot3(a_high, a_low, b_high, b_low):
    return dot(a_high, b_high) + (dot(a_high, b_low) + dot(a_low, b_high))


def coordinates():
    band = lax.axis_index("band")
    ga = lax.axis_index("ga")
    return band, ga // 8, (ga // 2) % 4, ga % 2


def device(band, z, y, c):
    return (band, z * 8 + y * 2 + c)


def greet(partners):
    barrier = pltpu.get_barrier_semaphore()
    for partner in partners:
        pl.semaphore_signal(barrier, inc=1, device_id=partner, device_id_type=MESH)
    pl.semaphore_wait(barrier, len(partners))


def send(src, dst, send_sem, recv_sem, partner):
    copy = pltpu.make_async_remote_copy(
        src_ref=src, dst_ref=dst, send_sem=send_sem, recv_sem=recv_sem, device_id=partner, device_id_type=MESH
    )
    copy.start()
    return copy


def density_step(first, step, chosen, pv_ref, pc_ref, dens):
    lanes = pl.ds(pl.multiple_of(step * 384, 384), 384)
    y2 = first + step
    for p in range(PAIRS):
        v, q = chosen[p]
        vr = pv_ref[0, v, :, lanes].astype(F32)
        vi = pv_ref[1, v, :, lanes].astype(F32)
        cr = pc_ref[0, q, :, lanes].astype(F32)
        ci = pc_ref[1, q, :, lanes].astype(F32)
        rows = slice(2 * p, 2 * p + 2)
        dens[y2, rows, 0:384] = vr * cr + vi * ci
        dens[y2, rows, 384:768] = vr * ci - vi * cr


def transform_planes(
    chosen, pv_refs, pc_refs, wzh_ref, wzl_ref, wyh_ref, wyl_ref, dens, zed, spec, wait_psi, wait_tables, after_density
):
    for piece in range(PIECES):
        wait_psi(piece)

        @pl.loop(0, HALF_Y // PIECES // 2)
        def _(step):
            for u in range(2):
                density_step(piece * (HALF_Y // PIECES), step * 2 + u, chosen, pv_refs[piece], pc_refs[piece], dens)

    after_density()
    wait_tables()
    for parity in range(2):
        first = 128 * parity
        both = jnp.concatenate([dens[:, :, first : first + 256], dens[:, :, 384 + first : 640 + first]], axis=2)
        high, low = split(both.reshape(768, 512))
        result = dot3(high, low, wzh_ref[parity], wzl_ref[parity])
        for tile in range(4):
            zed[parity, tile] = result[:, 128 * tile : 128 * tile + 128]
    for p in range(PAIRS):
        for plane in range(2):
            row = 2 * p + plane
            halves = [
                jnp.concatenate(
                    [
                        zed[parity, 2 * part + tile, pl.ds(row, HALF_Y, stride=16), :]
                        for part in range(2)
                        for parity in range(2)
                    ],
                    axis=0,
                )
                for tile in range(2)
            ]
            high, low = split(jnp.concatenate(halves, axis=1))
            result = dot3(wyh_ref[...], wyl_ref[...], high, low)
            for part in range(2):
                for tile in range(2):
                    spec[tile, pl.ds(part * 16 + plane * 8 + p, NY, stride=32), :] = result[
                        part * NY : (part + 1) * NY, 128 * tile : 128 * tile + 128
                    ]


def take(table, index):
    return jnp.take_along_axis(table, index, axis=1)


PICK = 384


def partial_block(m, cd, tiles, miller_of, table, plane_of_row, scale, spec, store):
    base = pl.multiple_of(m * 96, 96)
    line = miller_of(0, slice(0, G_DEV))
    second = line >= 96
    third = line >= 192
    sources = []
    for tile in range(3):
        k_row, half = (3 * cd + tile) // 2, (3 * cd + tile) % 2
        sources.append(spec[half, pl.ds(pl.multiple_of(base + 32 * k_row, 32), 32), :])
    if tiles[-1] * 128 >= PICK:
        key = line[:, PICK:] + jnp.where(third[:, PICK:], 64, jnp.where(second[:, PICK:], 32, 0))
        wide = G_DEV - PICK
        ones = jnp.where(
            lax.broadcasted_iota(jnp.int32, (384, wide), 0) == jnp.broadcast_to(key, (384, wide)), 1.0, 0.0
        ).astype(BF16)
        high, low = split(jnp.concatenate(sources, axis=1))
        picked = dot(jnp.concatenate([high, low], axis=0), ones)
        picked = picked[0:32] + picked[32:64]
    for g in tiles:
        lanes = slice(128 * g, 128 * g + 128)
        h = jnp.broadcast_to(miller_of(1, lanes), (8, 128))
        phases = take(table, (h * plane_of_row) & 127)
        c0, s0, c1, s1 = [jnp.broadcast_to(phases[i : i + 1], (8, 128)) for i in range(4)]
        got = []
        if 128 * g < PICK:
            in_second = jnp.broadcast_to(line[:, lanes], (8, 128)) >= 96
            in_third = jnp.broadcast_to(line[:, lanes], (8, 128)) >= 192
            index = jnp.broadcast_to(line[:, lanes], (8, 128)) - jnp.where(in_third, 192, jnp.where(in_second, 96, 0))
            for group in range(4):
                values = [take(source[8 * group : 8 * group + 8], index) for source in sources]
                got.append(jnp.where(in_third, values[2], jnp.where(in_second, values[1], values[0])))
        else:
            columns = slice(128 * g - PICK, 128 * g - PICK + 128)
            got = [picked[8 * group : 8 * group + 8, columns] for group in range(4)]
        re0, re1, im0, im1 = got
        out_re = (c0 * re0 + s0 * im0) + (c1 * re1 + s1 * im1)
        out_im = (c0 * im0 - s0 * re0) + (c1 * im1 - s1 * re1)
        store(slice(0, 8), lanes, out_re * scale)
        store(slice(8, 16), lanes, out_im * scale)


ROWS_AT = (2, 5, 9)
LAGS = (0, 2), (2, 0), (2, 2), (3, 2)
PIECES = 3
CHUNKS = 4
SLOTS = ZN // CHUNKS
FIRST = 3
OWN = ZN - FIRST


def main_kernel(
    pair_ref,
    val_ref,
    cond_ref,
    pv_hbm,
    pc_hbm,
    wzh_hbm,
    wzl_hbm,
    wyh_hbm,
    wyl_hbm,
    wx_ref,
    miller_ref,
    amps_ref,
    rows_ref,
    pv_refs,
    pc_refs,
    wzh_ref,
    wzl_ref,
    wyh_ref,
    wyl_ref,
    dens,
    zed,
    spec,
    lines,
    sums,
    from_core,
    relayed,
    near,
    far,
    total,
    by_z,
    amps,
    rows,
    x_out,
    x_in,
    z_out,
    z_in,
    load_sem,
    send_sem,
    recv_sem,
):
    band, z, y, c = coordinates()
    psi_loads = []
    for piece in range(PIECES):
        lanes = pl.ds(piece * (NY * NZ // PIECES), NY * NZ // PIECES)
        for n, (src, dst) in enumerate(((pv_hbm, pv_refs[piece]), (pc_hbm, pc_refs[piece]))):
            copy = pltpu.make_async_copy(src.at[:, :, :, lanes], dst, load_sem.at[2 * piece + n])
            copy.start()
            psi_loads.append(copy)
    table_loads = []
    for n, (src, dst) in enumerate(
        ((wzh_hbm, wzh_ref), (wzl_hbm, wzl_ref), (wyh_hbm, wyh_ref), (wyl_hbm, wyl_ref))
    ):
        copy = pltpu.make_async_copy(src, dst, load_sem.at[2 * PIECES + n])
        copy.start()
        table_loads.append(copy)

    def wait_psi(piece):
        for copy in psi_loads[2 * piece : 2 * piece + 2]:
            copy.wait()

    def wait_tables():
        for copy in table_loads:
            copy.wait()

    z_partners = [device(band, (z + d) % ZN, y, c) for d in range(1, ZN)]
    x_partners = [device((band + d) % BN, z, y, c) for d in range(1, BN)]
    core_partner = device(band, z, y, 1 - c)
    plane_partners = [core_partner] + [
        device(band, z, (y + d) % YN, (c + e) % CN) for d in range(1, YN) for e in range(CN)
    ]
    ahead = (y + 1 + 2 * c) % YN
    behind = (y + 3 - 2 * c) % YN
    across = (y + 2) % YN
    to_ahead = device(band, z, ahead, c)
    to_behind = device(band, z, behind, c)

    k = miller_ref[1:2, :]
    l = miller_ref[2:3, :]
    lines[z, y, c, 0:1, :] = jnp.where(k < 0, k + NY, k) * NZ + jnp.where(l < 0, l + NZ, l) - (z * 8 + y * 2 + c) * PENCILS
    lines[z, y, c, 1:2, :] = miller_ref[0:1, :] & (NX - 1)
    greet(z_partners + x_partners + plane_partners)

    sent = []

    def start(slot, src, dst, partner):
        copy = send(src, dst, send_sem.at[slot], recv_sem.at[slot], partner)
        sent.append(copy)
        return copy

    mine = lines.at[z, y, c]
    line_copies = [start(n, mine, mine, partner) for n, partner in enumerate(z_partners)]

    def pass_lines_on():
        for copy in line_copies:
            copy.wait_recv()
        block = lines.at[:, y, c]
        for n, partner in enumerate(plane_partners):
            line_copies.append(start(7 + n, block, block, partner))

    chosen = [(pair_ref[0, p] & 1, pair_ref[1, p] & 31) for p in range(PAIRS)]
    pair_rows = lax.broadcasted_iota(jnp.int32, (8, 128), 0)
    gap = jnp.ones((8, 128), F32)
    for p, (v, q) in enumerate(chosen):
        gap = jnp.where(pair_rows == p, cond_ref[q] - val_ref[v], gap)
    scale = jnp.sqrt(4.0 / (gap * math.sqrt(32.0)))
    plane_of_row = 2 * (z * 8 + y * 2 + c) + ((pair_rows >> 1) & 1)
    table = wx_ref[...]

    transform_planes(
        chosen, pv_refs, pc_refs, wzh_ref, wzl_ref, wyh_ref, wyl_ref, dens, zed, spec, wait_psi, wait_tables, pass_lines_on
    )
    for copy in line_copies[7:]:
        copy.wait_recv()

    def place(n):
        return jnp.where(n == 0, across, jnp.where(n == 1, ahead, jnp.where(n == 2, behind, y)))

    def part(ref, chunk, *index):
        return ref.at[(*index, pl.ds(chunk * SLOTS, SLOTS), slice(None), pl.ds(128, G_DEV - 128))]

    def early(ref, *index):
        return ref.at[(*index, slice(None), slice(None), pl.ds(0, 128))]

    def remote(slot, src, dst, partner):
        return pltpu.make_async_remote_copy(
            src_ref=src,
            dst_ref=dst,
            send_sem=send_sem.at[slot],
            recv_sem=recv_sem.at[slot],
            device_id=partner,
            device_id_type=MESH,
        )

    def core_copy(n, chunk):
        yd = place(n)
        return remote(14 + 7 * chunk + n, part(sums, chunk, 1 - c, yd), part(from_core, chunk, yd), core_partner)

    def relay_copy(chunk):
        return remote(14 + 7 * chunk + 4, part(from_core, chunk, across), part(relayed, chunk), to_ahead)

    def back_copy(chunk):
        return remote(14 + 7 * chunk + 5, part(from_core, chunk, behind), part(near, chunk), to_behind)

    def forth_copy(chunk):
        return remote(14 + 7 * chunk + 6, part(from_core, chunk, ahead), part(far, chunk), to_ahead)

    along_z = 14 + 7 * CHUNKS

    def z_copy(slot):
        return remote(
            along_z + slot, total.at[slot], by_z.at[slot], device(band, (z + slot + FIRST) % ZN, y, c)
        )

    def join(n, chunk, yd):
        core_copy(n, chunk).wait_recv()
        part(from_core, chunk, yd)[...] += part(sums, chunk, c, yd)[...]

    def send_relay(chunk):
        join(0, chunk, across)
        relay_copy(chunk).start()

    def send_back(chunk):
        join(1, chunk, behind)
        back_copy(chunk).start()

    def send_forth(chunk):
        join(2, chunk, ahead)
        relay_copy(chunk).wait_recv()
        part(from_core, chunk, ahead)[...] += part(relayed, chunk)[...]
        forth_copy(chunk).start()

    def send_z(chunk):
        core_copy(3, chunk).wait_recv()
        part(total, chunk)[...] = part(from_core, chunk, y)[...] + part(sums, chunk, c, y)[...]
        back_copy(chunk).wait_recv()
        forth_copy(chunk).wait_recv()
        part(total, chunk)[...] += part(near, chunk)[...] + part(far, chunk)[...]
        for i in range(SLOTS):
            slot = chunk * SLOTS + i

            @pl.when(slot != OWN)
            def _():
                z_copy(slot).start()

    steps = 4 * CHUNKS
    actions = [(n * CHUNKS + lag, action) for (n, lag), action in zip(LAGS, (send_relay, send_back, send_forth, send_z))]

    def add_up(n, slots, tiles):
        yd = place(n)
        for slot in slots:
            zd = (z + slot + FIRST) % ZN
            for cd in range(CN):

                def miller_of(kind, lanes):
                    return lines[zd, yd, cd, kind : kind + 1, lanes]

                def store(sublanes, lanes, value):
                    sums[cd, yd, slot, sublanes, lanes] = value

                partial_block(zd * YN + yd, cd, tiles, miller_of, table, plane_of_row, scale, spec, store)

    x_rows = along_z + 8
    z_rows = x_rows + 3
    plane_rows = z_rows + 7
    along_x = plane_rows + 7
    early_at = along_x + 3

    def early_core(n):
        yd = place(n)
        return remote(early_at + n, early(sums, 1 - c, yd), early(from_core, yd), core_partner)

    def early_join(n, yd):
        early_core(n).wait_recv()
        early(from_core, yd)[...] += early(sums, c, yd)[...]

    early_relay = remote(early_at + 4, early(from_core, across), early(relayed), to_ahead)
    early_back = remote(early_at + 5, early(from_core, behind), early(near), to_behind)
    early_forth = remote(early_at + 6, early(from_core, ahead), early(far), to_ahead)

    @pl.loop(0, 4)
    def _(n):
        @pl.loop(0, 2)
        def _(half):
            add_up(n, [half * 4 + i for i in range(4)], [0])

        early_core(n).start()

    early_join(0, across)
    early_relay.start()
    early_join(1, behind)
    early_back.start()

    def own_rows(to_band, z2):
        return total[(2 * to_band + z2 - z - FIRST + 2 * ZN) % ZN, :, 0:128]

    x_row_copies = [remote(x_rows + n, x_out.at[n], x_in.at[band], partner) for n, partner in enumerate(x_partners)]
    z_row_copies = [remote(z_rows + n, z_out, z_in.at[n], partner) for n, partner in enumerate(z_partners)]

    def rows_y():
        early_join(2, ahead)
        early_relay.wait_recv()
        early(from_core, ahead)[...] += early(relayed)[...]
        early_forth.start()

    def rows_x():
        early_core(3).wait_recv()
        early_back.wait_recv()
        early_forth.wait_recv()
        early(total)[...] = (early(from_core, y)[...] + early(sums, c, y)[...]) + (early(near)[...] + early(far)[...])
        for n in range(BN - 1):
            for z2 in range(2):
                x_out[n, z2] = own_rows((band + n + 1) % BN, z2)
            x_row_copies[n].start()
        for z2 in range(2):
            x_in[band, z2] = own_rows(band, z2)

    def rows_z():
        for copy in x_row_copies:
            copy.wait_recv()
        for z2 in range(2):
            parts = [x_in[b, z2] for b in range(BN)]
            for_real = [-piece for piece in parts]
            for_imag = [piece for both in parts for piece in (-both[8:16], both[0:8])]
            z_out[z2] = jnp.concatenate(for_real + for_imag, axis=0).T[0:ROW_DEV]
        for copy in z_row_copies:
            copy.start()

    @pl.loop(0, steps)
    def _(step):
        n = step // CHUNKS
        chunk = step % CHUNKS
        add_up(n, [chunk * SLOTS + i for i in range(SLOTS)], [1, 2, 3, 4])
        core_copy(n, chunk).start()
        for at, action in zip(ROWS_AT, (rows_y, rows_x, rows_z)):
            pl.when(step == at)(action)
        for first, action in actions:

            @pl.when((step >= first) & (step < first + CHUNKS))
            def _():
                action(step - first)

    for step in range(steps, steps + 2 * CHUNKS):
        for first, action in actions:
            if first <= step < first + CHUNKS:
                action(step - first)

    own = z_out[...]
    for n, copy in enumerate(z_row_copies):
        copy.wait_recv()
        own = own + z_in[n]
    for z2 in range(2):
        rows[z2, y, c] = own[z2]
    block = rows.at[:, y, c]
    row_copies = [start(plane_rows + n, block, block, partner) for n, partner in enumerate(plane_partners)]
    result = total[OWN]
    for slot in range(ZN):
        if slot != OWN:
            z_copy(slot).wait_recv()
            result = result + by_z[slot]
    amps[band] = result
    amp_copies = [
        start(along_x + n, amps.at[band], amps.at[band], partner) for n, partner in enumerate(x_partners)
    ]
    for copy in amp_copies:
        copy.wait_recv()
    amps_ref[...] = amps[...]
    for copy in row_copies:
        copy.wait_recv()
    rows_ref[...] = rows[...]
    for copy in sent:
        copy.wait_send()
    for chunk in range(CHUNKS):
        for copy in [core_copy(n, chunk) for n in range(4)] + [relay_copy(chunk), back_copy(chunk), forth_copy(chunk)]:
            copy.wait_send()
    for slot in range(ZN):
        if slot != OWN:
            z_copy(slot).wait_send()
    for copy in [early_core(n) for n in range(4)] + [early_relay, early_back, early_forth] + x_row_copies + z_row_copies:
        copy.wait_send()


def amplitudes(pair_list, val_energy, cond_energy, psi_valence, psi_conduction, miller):
    vmem = pl.BlockSpec(memory_space=pltpu.VMEM)
    smem = pl.BlockSpec(memory_space=pltpu.SMEM)
    wzh, wzl = split_np(z_table())
    wyh, wyl = split_np(y_table())
    tables = [jnp.asarray(t) for t in (wzh, wzl, wyh, wyl, x_table())]
    block = (ZN, 16, G_DEV)
    return pl.pallas_call(
        main_kernel,
        out_shape=(
            jax.ShapeDtypeStruct((BN, 16, G_DEV), F32),
            jax.ShapeDtypeStruct((2, YN, CN, ROW_DEV, 128), F32),
        ),
        in_specs=[smem] * 3 + [pl.BlockSpec(memory_space=pl.ANY)] * 6 + [vmem] * 2,
        out_specs=(vmem, vmem),
        scratch_shapes=[
            [pltpu.VMEM((2, 2, 2, NY * NZ // PIECES), BF16)] * PIECES,
            [pltpu.VMEM((2, 32, 2, NY * NZ // PIECES), BF16)] * PIECES,
            pltpu.VMEM(wzh.shape, BF16),
            pltpu.VMEM(wzl.shape, BF16),
            pltpu.VMEM(wyh.shape, BF16),
            pltpu.VMEM(wyl.shape, BF16),
            pltpu.VMEM((HALF_Y, 16, 768), F32),
            pltpu.VMEM((2, 4, 768, 128), F32),
            pltpu.VMEM((2, NY * 32, 128), F32),
            pltpu.VMEM((ZN, YN, CN, 2, G_DEV), jnp.int32),
            pltpu.VMEM((CN, YN) + block, F32),
            pltpu.VMEM((YN,) + block, F32),
            pltpu.VMEM(block, F32),
            pltpu.VMEM(block, F32),
            pltpu.VMEM(block, F32),
            pltpu.VMEM(block, F32),
            pltpu.VMEM(block, F32),
            pltpu.VMEM((BN, 16, G_DEV), F32),
            pltpu.VMEM((2, YN, CN, ROW_DEV, 128), F32),
            pltpu.VMEM((BN - 1, 2, 16, 128), F32),
            pltpu.VMEM((BN, 2, 16, 128), F32),
            pltpu.VMEM((2, ROW_DEV, 128), F32),
            pltpu.VMEM((ZN - 1, 2, ROW_DEV, 128), F32),
            pltpu.SemaphoreType.DMA((2 * PIECES + 4,)),
            pltpu.SemaphoreType.DMA((14 + 7 * CHUNKS + 35,)),
            pltpu.SemaphoreType.DMA((14 + 7 * CHUNKS + 35,)),
        ],
        compiler_params=pltpu.CompilerParams(
            collective_id=0, has_side_effects=True, vmem_limit_bytes=56 * 1024 * 1024
        ),
        name="amplitudes",
    )(pair_list, val_energy, cond_energy, psi_valence, psi_conduction, *tables, miller)


def slab_kernel(rows_ref, amps_ref, out_ref):
    right_high, right_low = split(amps_ref[...].reshape(64, G_DEV))
    for part in range(2):
        left = rows_ref[...].reshape(256, 128)[:, 64 * part : 64 * part + 64]
        left_high, left_low = split(left)
        out_ref[:, part, :] = dot3(left_high, left_low, right_high, right_low)


def slab(rows, amps):
    vmem = pl.BlockSpec(memory_space=pltpu.VMEM)
    return pl.pallas_call(
        slab_kernel,
        out_shape=jax.ShapeDtypeStruct((256, 2, G_DEV), F32),
        in_specs=[vmem, vmem],
        out_specs=vmem,
        compiler_params=pltpu.CompilerParams(vmem_limit_bytes=60 * 1024 * 1024),
        name="slab",
    )(rows, amps)


def per_device(psi_valence, psi_conduction, val_energy, cond_energy, miller, pair_list):
    amps, rows = amplitudes(pair_list, val_energy, cond_energy, psi_valence, psi_conduction, miller)
    return slab(rows, amps)


def solution(mesh):
    return jax.shard_map(
        per_device,
        mesh=mesh,
        in_specs=(
            P(None, None, "ga", None),
            P(None, "band", "ga", None),
            P(),
            P("band"),
            P(None, "ga"),
            P(None, "band"),
        ),
        out_specs=P("band", None, "ga"),
        check_vma=False,
    )
```

```python
import math

import jax
import jax.numpy as jnp
import numpy as np
from jax import lax
from jax.experimental import pallas as pl
from jax.experimental.pallas import tpu as pltpu
from jax.sharding import PartitionSpec as P

NX = 128
NY = 96
NZ = 192
ROW_DEV = 16
PAIRS = 8
GA = 64
ZN, YN, CN, BN = 8, 4, 2, 4
HALF_Y = NY // 2
PENCILS = NY * NZ // GA
G_DEV = 640
TILES = G_DEV // 128
MESH = pl.DeviceIdType.MESH
F32 = jnp.float32
BF16 = jnp.bfloat16


def split_np(table):
    high = table.astype(np.float32).astype(jnp.bfloat16)
    low = (table - high.astype(np.float64)).astype(jnp.bfloat16)
    return high, low


def z_table():
    points = np.arange(NZ)
    angle = 2.0 * np.pi * ((points[:, None] * points[None, :]) % NZ) / NZ
    cosine, sine = np.cos(angle), np.sin(angle)
    table = np.zeros((2, 2, 256, 2, 2, 128))
    for parity in range(2):
        rows = slice(64 * parity, 64 * parity + NZ)
        for part_in in range(2):
            for part_out in range(2):
                values = cosine if part_in == part_out else (sine if part_in else -sine)
                for half in range(2):
                    table[parity, part_in, rows, part_out, half, 0:96] = values[:, 96 * half : 96 * half + 96]
    return table.reshape(2, 512, 512)


def y_table():
    k = np.arange(NY)[:, None]
    table = np.zeros((2, NY, 2, 2, HALF_Y))
    for parity in range(2):
        y = 2 * np.arange(HALF_Y)[None, :] + parity
        angle = 2.0 * np.pi * ((k * y) % NY) / NY
        table[0, :, 0, parity] = np.cos(angle)
        table[0, :, 1, parity] = np.sin(angle)
        table[1, :, 0, parity] = -np.sin(angle)
        table[1, :, 1, parity] = np.cos(angle)
    return table.reshape(2 * NY, 4 * HALF_Y)


def x_table():
    angle = 2.0 * np.pi * np.arange(NX) / NX
    norm = 1.0 / math.sqrt(NX * NY * NZ)
    return np.tile(np.stack([np.cos(angle), np.sin(angle)]) * norm, (4, 1)).astype(np.float32)


def split(value):
    high = value.astype(BF16)
    low = (value - high.astype(F32)).astype(BF16)
    return high, low


def dot(a, b):
    return jnp.dot(a, b, preferred_element_type=F32)


def dot3(a_high, a_low, b_high, b_low):
    return dot(a_high, b_high) + (dot(a_high, b_low) + dot(a_low, b_high))


def coordinates():
    band = lax.axis_index("band")
    ga = lax.axis_index("ga")
    return band, ga // 8, (ga // 2) % 4, ga % 2


def device(band, z, y, c):
    return (band, z * 8 + y * 2 + c)


def greet(partners):
    barrier = pltpu.get_barrier_semaphore()
    for partner in partners:
        pl.semaphore_signal(barrier, inc=1, device_id=partner, device_id_type=MESH)
    return lambda: pl.semaphore_wait(barrier, len(partners))


def send(src, dst, send_sem, recv_sem, partner):
    copy = pltpu.make_async_remote_copy(
        src_ref=src, dst_ref=dst, send_sem=send_sem, recv_sem=recv_sem, device_id=partner, device_id_type=MESH
    )
    copy.start()
    return copy


def density_step(first, step, chosen, pv_ref, pc_ref, dens):
    lanes = pl.ds(pl.multiple_of(step * 384, 384), 384)
    y2 = first + step
    for p in range(PAIRS):
        v, q = chosen[p]
        vr = pv_ref[0, v, :, lanes].astype(F32)
        vi = pv_ref[1, v, :, lanes].astype(F32)
        cr = pc_ref[0, q, :, lanes].astype(F32)
        ci = pc_ref[1, q, :, lanes].astype(F32)
        rows = slice(2 * p, 2 * p + 2)
        dens[y2, rows, 0:384] = vr * cr + vi * ci
        dens[y2, rows, 384:768] = vr * ci - vi * cr


def transform_planes(
    chosen, pv_refs, pc_refs, wzh_ref, wzl_ref, wyh_ref, wyl_ref, dens, zed, spec, wait_psi, wait_tables, after_density
):
    for piece in range(PIECES):
        wait_psi(piece)

        @pl.loop(0, HALF_Y // PIECES // 2)
        def _(step):
            for u in range(2):
                density_step(piece * (HALF_Y // PIECES), step * 2 + u, chosen, pv_refs[piece], pc_refs[piece], dens)

    after_density()
    wait_tables()
    for parity in range(2):
        first = 128 * parity
        both = jnp.concatenate([dens[:, :, first : first + 256], dens[:, :, 384 + first : 640 + first]], axis=2)
        high, low = split(both.reshape(768, 512))
        result = dot3(high, low, wzh_ref[parity], wzl_ref[parity])
        for tile in range(4):
            zed[parity, tile] = result[:, 128 * tile : 128 * tile + 128]
    for p in range(PAIRS):
        for plane in range(2):
            row = 2 * p + plane
            halves = [
                jnp.concatenate(
                    [
                        zed[parity, 2 * part + tile, pl.ds(row, HALF_Y, stride=16), :]
                        for part in range(2)
                        for parity in range(2)
                    ],
                    axis=0,
                )
                for tile in range(2)
            ]
            high, low = split(jnp.concatenate(halves, axis=1))
            result = dot3(wyh_ref[...], wyl_ref[...], high, low)
            for part in range(2):
                for tile in range(2):
                    spec[tile, pl.ds(part * 16 + plane * 8 + p, NY, stride=32), :] = result[
                        part * NY : (part + 1) * NY, 128 * tile : 128 * tile + 128
                    ]


def take(table, index):
    return jnp.take_along_axis(table, index, axis=1)


PICK = 384


def partial_block(m, cd, tiles, miller_of, table, plane_of_row, scale, spec, store):
    base = pl.multiple_of(m * 96, 96)
    line = miller_of(0, slice(0, G_DEV))
    second = line >= 96
    third = line >= 192
    sources = []
    for tile in range(3):
        k_row, half = (3 * cd + tile) // 2, (3 * cd + tile) % 2
        sources.append(spec[half, pl.ds(pl.multiple_of(base + 32 * k_row, 32), 32), :])
    if tiles[-1] * 128 >= PICK:
        key = line[:, PICK:] + jnp.where(third[:, PICK:], 64, jnp.where(second[:, PICK:], 32, 0))
        wide = G_DEV - PICK
        ones = jnp.where(
            lax.broadcasted_iota(jnp.int32, (384, wide), 0) == jnp.broadcast_to(key, (384, wide)), 1.0, 0.0
        ).astype(BF16)
        high, low = split(jnp.concatenate(sources, axis=1))
        picked = dot(jnp.concatenate([high, low], axis=0), ones)
        picked = picked[0:32] + picked[32:64]
    for g in tiles:
        lanes = slice(128 * g, 128 * g + 128)
        h = jnp.broadcast_to(miller_of(1, lanes), (8, 128))
        phases = take(table, (h * plane_of_row) & 127)
        c0, s0, c1, s1 = [jnp.broadcast_to(phases[i : i + 1], (8, 128)) for i in range(4)]
        got = []
        if 128 * g < PICK:
            in_second = jnp.broadcast_to(line[:, lanes], (8, 128)) >= 96
            in_third = jnp.broadcast_to(line[:, lanes], (8, 128)) >= 192
            index = jnp.broadcast_to(line[:, lanes], (8, 128)) - jnp.where(in_third, 192, jnp.where(in_second, 96, 0))
            for group in range(4):
                values = [take(source[8 * group : 8 * group + 8], index) for source in sources]
                got.append(jnp.where(in_third, values[2], jnp.where(in_second, values[1], values[0])))
        else:
            columns = slice(128 * g - PICK, 128 * g - PICK + 128)
            got = [picked[8 * group : 8 * group + 8, columns] for group in range(4)]
        re0, re1, im0, im1 = got
        out_re = (c0 * re0 + s0 * im0) + (c1 * re1 + s1 * im1)
        out_im = (c0 * im0 - s0 * re0) + (c1 * im1 - s1 * re1)
        store(slice(0, 8), lanes, out_re * scale)
        store(slice(8, 16), lanes, out_im * scale)


ROWS_AT = (2, 5, 9)
LAGS = (0, 2), (2, 0), (2, 2), (3, 2)
PIECES = 3
CHUNKS = 4
SLOTS = ZN // CHUNKS
FIRST = 3
OWN = ZN - FIRST


def main_kernel(
    pair_ref,
    val_ref,
    cond_ref,
    pv_hbm,
    pc_hbm,
    wzh_hbm,
    wzl_hbm,
    wyh_hbm,
    wyl_hbm,
    wx_ref,
    miller_ref,
    amps_ref,
    rows_ref,
    pv_refs,
    pc_refs,
    wzh_ref,
    wzl_ref,
    wyh_ref,
    wyl_ref,
    dens,
    zed,
    spec,
    lines,
    sums,
    from_core,
    relayed,
    near,
    far,
    total,
    by_z,
    amps,
    rows,
    x_out,
    x_in,
    z_out,
    z_in,
    load_sem,
    send_sem,
    recv_sem,
):
    band, z, y, c = coordinates()
    z_partners = [device(band, (z + d) % ZN, y, c) for d in range(1, ZN)]
    x_partners = [device((band + d) % BN, z, y, c) for d in range(1, BN)]
    core_partner = device(band, z, y, 1 - c)
    plane_partners = [core_partner] + [
        device(band, z, (y + d) % YN, (c + e) % CN) for d in range(1, YN) for e in range(CN)
    ]
    wait_for_partners = greet(z_partners + x_partners + plane_partners)
    psi_loads = []
    for piece in range(PIECES):
        lanes = pl.ds(piece * (NY * NZ // PIECES), NY * NZ // PIECES)
        for n, (src, dst) in enumerate(((pv_hbm, pv_refs[piece]), (pc_hbm, pc_refs[piece]))):
            copy = pltpu.make_async_copy(src.at[:, :, :, lanes], dst, load_sem.at[2 * piece + n])
            copy.start()
            psi_loads.append(copy)
    table_loads = []
    for n, (src, dst) in enumerate(
        ((wzh_hbm, wzh_ref), (wzl_hbm, wzl_ref), (wyh_hbm, wyh_ref), (wyl_hbm, wyl_ref))
    ):
        copy = pltpu.make_async_copy(src, dst, load_sem.at[2 * PIECES + n])
        copy.start()
        table_loads.append(copy)

    def wait_psi(piece):
        for copy in psi_loads[2 * piece : 2 * piece + 2]:
            copy.wait()

    def wait_tables():
        for copy in table_loads:
            copy.wait()

    ahead = (y + 1 + 2 * c) % YN
    behind = (y + 3 - 2 * c) % YN
    across = (y + 2) % YN
    to_ahead = device(band, z, ahead, c)
    to_behind = device(band, z, behind, c)

    k = miller_ref[1:2, :]
    l = miller_ref[2:3, :]
    lines[z, y, c, 0:1, :] = jnp.where(k < 0, k + NY, k) * NZ + jnp.where(l < 0, l + NZ, l) - (z * 8 + y * 2 + c) * PENCILS
    lines[z, y, c, 1:2, :] = miller_ref[0:1, :] & (NX - 1)
    wait_for_partners()

    sent = []

    def start(slot, src, dst, partner):
        copy = send(src, dst, send_sem.at[slot], recv_sem.at[slot], partner)
        sent.append(copy)
        return copy

    mine = lines.at[z, y, c]
    line_copies = [start(n, mine, mine, partner) for n, partner in enumerate(z_partners)]

    def pass_lines_on():
        for copy in line_copies:
            copy.wait_recv()
        block = lines.at[:, y, c]
        for n, partner in enumerate(plane_partners):
            line_copies.append(start(7 + n, block, block, partner))

    chosen = [(pair_ref[0, p] & 1, pair_ref[1, p] & 31) for p in range(PAIRS)]
    pair_rows = lax.broadcasted_iota(jnp.int32, (8, 128), 0)
    gap = jnp.ones((8, 128), F32)
    for p, (v, q) in enumerate(chosen):
        gap = jnp.where(pair_rows == p, cond_ref[q] - val_ref[v], gap)
    scale = jnp.sqrt(4.0 / (gap * math.sqrt(32.0)))
    plane_of_row = 2 * (z * 8 + y * 2 + c) + ((pair_rows >> 1) & 1)
    table = wx_ref[...]

    transform_planes(
        chosen, pv_refs, pc_refs, wzh_ref, wzl_ref, wyh_ref, wyl_ref, dens, zed, spec, wait_psi, wait_tables, pass_lines_on
    )
    for copy in line_copies[7:]:
        copy.wait_recv()

    def place(n):
        return jnp.where(n == 0, across, jnp.where(n == 1, ahead, jnp.where(n == 2, behind, y)))

    def part(ref, chunk, *index):
        return ref.at[(*index, pl.ds(chunk * SLOTS, SLOTS), slice(None), pl.ds(128, G_DEV - 128))]

    def early(ref, *index):
        return ref.at[(*index, slice(None), slice(None), pl.ds(0, 128))]

    def remote(slot, src, dst, partner):
        return pltpu.make_async_remote_copy(
            src_ref=src,
            dst_ref=dst,
            send_sem=send_sem.at[slot],
            recv_sem=recv_sem.at[slot],
            device_id=partner,
            device_id_type=MESH,
        )

    def core_copy(n, chunk):
        yd = place(n)
        return remote(14 + 7 * chunk + n, part(sums, chunk, 1 - c, yd), part(from_core, chunk, yd), core_partner)

    def relay_copy(chunk):
        return remote(14 + 7 * chunk + 4, part(from_core, chunk, across), part(relayed, chunk), to_ahead)

    def back_copy(chunk):
        return remote(14 + 7 * chunk + 5, part(from_core, chunk, behind), part(near, chunk), to_behind)

    def forth_copy(chunk):
        return remote(14 + 7 * chunk + 6, part(from_core, chunk, ahead), part(far, chunk), to_ahead)

    along_z = 14 + 7 * CHUNKS

    def z_copy(slot):
        return remote(
            along_z + slot, total.at[slot], by_z.at[slot], device(band, (z + slot + FIRST) % ZN, y, c)
        )

    def join(n, chunk, yd):
        core_copy(n, chunk).wait_recv()
        part(from_core, chunk, yd)[...] += part(sums, chunk, c, yd)[...]

    def send_relay(chunk):
        join(0, chunk, across)
        relay_copy(chunk).start()

    def send_back(chunk):
        join(1, chunk, behind)
        back_copy(chunk).start()

    def send_forth(chunk):
        join(2, chunk, ahead)
        relay_copy(chunk).wait_recv()
        part(from_core, chunk, ahead)[...] += part(relayed, chunk)[...]
        forth_copy(chunk).start()

    def send_z(chunk):
        core_copy(3, chunk).wait_recv()
        part(total, chunk)[...] = part(from_core, chunk, y)[...] + part(sums, chunk, c, y)[...]
        back_copy(chunk).wait_recv()
        forth_copy(chunk).wait_recv()
        part(total, chunk)[...] += part(near, chunk)[...] + part(far, chunk)[...]
        for i in range(SLOTS):
            slot = chunk * SLOTS + i

            @pl.when(slot != OWN)
            def _():
                z_copy(slot).start()

    steps = 4 * CHUNKS
    actions = [(n * CHUNKS + lag, action) for (n, lag), action in zip(LAGS, (send_relay, send_back, send_forth, send_z))]

    def add_up(n, slots, tiles):
        yd = place(n)
        for slot in slots:
            zd = (z + slot + FIRST) % ZN
            for cd in range(CN):

                def miller_of(kind, lanes):
                    return lines[zd, yd, cd, kind : kind + 1, lanes]

                def store(sublanes, lanes, value):
                    sums[cd, yd, slot, sublanes, lanes] = value

                partial_block(zd * YN + yd, cd, tiles, miller_of, table, plane_of_row, scale, spec, store)

    x_rows = along_z + 8
    z_rows = x_rows + 3
    plane_rows = z_rows + 7
    along_x = plane_rows + 7
    early_at = along_x + 3

    def early_core(n):
        yd = place(n)
        return remote(early_at + n, early(sums, 1 - c, yd), early(from_core, yd), core_partner)

    def early_join(n, yd):
        early_core(n).wait_recv()
        early(from_core, yd)[...] += early(sums, c, yd)[...]

    early_relay = remote(early_at + 4, early(from_core, across), early(relayed), to_ahead)
    early_back = remote(early_at + 5, early(from_core, behind), early(near), to_behind)
    early_forth = remote(early_at + 6, early(from_core, ahead), early(far), to_ahead)

    @pl.loop(0, 4)
    def _(n):
        @pl.loop(0, 2)
        def _(half):
            add_up(n, [half * 4 + i for i in range(4)], [0])

        early_core(n).start()

    early_join(0, across)
    early_relay.start()
    early_join(1, behind)
    early_back.start()

    def own_rows(to_band, z2):
        return total[(2 * to_band + z2 - z - FIRST + 2 * ZN) % ZN, :, 0:128]

    x_row_copies = [remote(x_rows + n, x_out.at[n], x_in.at[band], partner) for n, partner in enumerate(x_partners)]
    z_row_copies = [remote(z_rows + n, z_out, z_in.at[n], partner) for n, partner in enumerate(z_partners)]

    def rows_y():
        early_join(2, ahead)
        early_relay.wait_recv()
        early(from_core, ahead)[...] += early(relayed)[...]
        early_forth.start()

    def rows_x():
        early_core(3).wait_recv()
        early_back.wait_recv()
        early_forth.wait_recv()
        early(total)[...] = (early(from_core, y)[...] + early(sums, c, y)[...]) + (early(near)[...] + early(far)[...])
        for n in range(BN - 1):
            for z2 in range(2):
                x_out[n, z2] = own_rows((band + n + 1) % BN, z2)
            x_row_copies[n].start()
        for z2 in range(2):
            x_in[band, z2] = own_rows(band, z2)

    def rows_z():
        for copy in x_row_copies:
            copy.wait_recv()
        for z2 in range(2):
            parts = [x_in[b, z2] for b in range(BN)]
            for_real = [-piece for piece in parts]
            for_imag = [piece for both in parts for piece in (-both[8:16], both[0:8])]
            z_out[z2] = jnp.concatenate(for_real + for_imag, axis=0).T[0:ROW_DEV]
        for copy in z_row_copies:
            copy.start()

    @pl.loop(0, steps)
    def _(step):
        n = step // CHUNKS
        chunk = step % CHUNKS
        add_up(n, [chunk * SLOTS + i for i in range(SLOTS)], [1, 2, 3, 4])
        core_copy(n, chunk).start()
        for at, action in zip(ROWS_AT, (rows_y, rows_x, rows_z)):
            pl.when(step == at)(action)
        for first, action in actions:

            @pl.when((step >= first) & (step < first + CHUNKS))
            def _():
                action(step - first)

    for step in range(steps, steps + 2 * CHUNKS):
        for first, action in actions:
            if first <= step < first + CHUNKS:
                action(step - first)

    own = z_out[...]
    for n, copy in enumerate(z_row_copies):
        copy.wait_recv()
        own = own + z_in[n]
    for z2 in range(2):
        rows[z2, y, c] = own[z2]
    block = rows.at[:, y, c]
    row_copies = [start(plane_rows + n, block, block, partner) for n, partner in enumerate(plane_partners)]
    result = total[OWN]
    for slot in range(ZN):
        if slot != OWN:
            z_copy(slot).wait_recv()
            result = result + by_z[slot]
    amps[band] = result
    amp_copies = [
        start(along_x + n, amps.at[band], amps.at[band], partner) for n, partner in enumerate(x_partners)
    ]
    for copy in amp_copies:
        copy.wait_recv()
    amps_ref[...] = amps[...]
    for copy in row_copies:
        copy.wait_recv()
    rows_ref[...] = rows[...]
    for copy in sent:
        copy.wait_send()
    for chunk in range(CHUNKS):
        for copy in [core_copy(n, chunk) for n in range(4)] + [relay_copy(chunk), back_copy(chunk), forth_copy(chunk)]:
            copy.wait_send()
    for slot in range(ZN):
        if slot != OWN:
            z_copy(slot).wait_send()
    for copy in [early_core(n) for n in range(4)] + [early_relay, early_back, early_forth] + x_row_copies + z_row_copies:
        copy.wait_send()


def amplitudes(pair_list, val_energy, cond_energy, psi_valence, psi_conduction, miller):
    vmem = pl.BlockSpec(memory_space=pltpu.VMEM)
    smem = pl.BlockSpec(memory_space=pltpu.SMEM)
    wzh, wzl = split_np(z_table())
    wyh, wyl = split_np(y_table())
    tables = [jnp.asarray(t) for t in (wzh, wzl, wyh, wyl, x_table())]
    block = (ZN, 16, G_DEV)
    return pl.pallas_call(
        main_kernel,
        out_shape=(
            jax.ShapeDtypeStruct((BN, 16, G_DEV), F32),
            jax.ShapeDtypeStruct((2, YN, CN, ROW_DEV, 128), F32),
        ),
        in_specs=[smem] * 3 + [pl.BlockSpec(memory_space=pl.ANY)] * 6 + [vmem] * 2,
        out_specs=(vmem, vmem),
        scratch_shapes=[
            [pltpu.VMEM((2, 2, 2, NY * NZ // PIECES), BF16)] * PIECES,
            [pltpu.VMEM((2, 32, 2, NY * NZ // PIECES), BF16)] * PIECES,
            pltpu.VMEM(wzh.shape, BF16),
            pltpu.VMEM(wzl.shape, BF16),
            pltpu.VMEM(wyh.shape, BF16),
            pltpu.VMEM(wyl.shape, BF16),
            pltpu.VMEM((HALF_Y, 16, 768), F32),
            pltpu.VMEM((2, 4, 768, 128), F32),
            pltpu.VMEM((2, NY * 32, 128), F32),
            pltpu.VMEM((ZN, YN, CN, 2, G_DEV), jnp.int32),
            pltpu.VMEM((CN, YN) + block, F32),
            pltpu.VMEM((YN,) + block, F32),
            pltpu.VMEM(block, F32),
            pltpu.VMEM(block, F32),
            pltpu.VMEM(block, F32),
            pltpu.VMEM(block, F32),
            pltpu.VMEM(block, F32),
            pltpu.VMEM((BN, 16, G_DEV), F32),
            pltpu.VMEM((2, YN, CN, ROW_DEV, 128), F32),
            pltpu.VMEM((BN - 1, 2, 16, 128), F32),
            pltpu.VMEM((BN, 2, 16, 128), F32),
            pltpu.VMEM((2, ROW_DEV, 128), F32),
            pltpu.VMEM((ZN - 1, 2, ROW_DEV, 128), F32),
            pltpu.SemaphoreType.DMA((2 * PIECES + 4,)),
            pltpu.SemaphoreType.DMA((14 + 7 * CHUNKS + 35,)),
            pltpu.SemaphoreType.DMA((14 + 7 * CHUNKS + 35,)),
        ],
        compiler_params=pltpu.CompilerParams(
            collective_id=0, has_side_effects=True, vmem_limit_bytes=56 * 1024 * 1024
        ),
        name="amplitudes",
    )(pair_list, val_energy, cond_energy, psi_valence, psi_conduction, *tables, miller)


def slab_kernel(rows_ref, amps_ref, out_ref):
    right_high, right_low = split(amps_ref[...].reshape(64, G_DEV))
    right = jnp.concatenate([right_high, right_low, right_high], axis=0)
    for part in range(2):
        left_high, left_low = split(rows_ref[...].reshape(256, 128)[:, 64 * part : 64 * part + 64])
        out_ref[:, part, :] = dot(jnp.concatenate([left_high, left_high, left_low], axis=1), right)


def slab(rows, amps):
    vmem = pl.BlockSpec(memory_space=pltpu.VMEM)
    return pl.pallas_call(
        slab_kernel,
        out_shape=jax.ShapeDtypeStruct((256, 2, G_DEV), F32),
        in_specs=[vmem, vmem],
        out_specs=vmem,
        compiler_params=pltpu.CompilerParams(vmem_limit_bytes=60 * 1024 * 1024),
        name="slab",
    )(rows, amps)


def per_device(psi_valence, psi_conduction, val_energy, cond_energy, miller, pair_list):
    amps, rows = amplitudes(pair_list, val_energy, cond_energy, psi_valence, psi_conduction, miller)
    return slab(rows, amps)


def solution(mesh):
    return jax.shard_map(
        per_device,
        mesh=mesh,
        in_specs=(
            P(None, None, "ga", None),
            P(None, "band", "ga", None),
            P(),
            P("band"),
            P(None, "ga"),
            P(None, "band"),
        ),
        out_specs=P("band", None, "ga"),
        check_vma=False,
    )
```

```python
import math

import jax
import jax.numpy as jnp
import numpy as np
from jax import lax
from jax.experimental import pallas as pl
from jax.experimental.pallas import tpu as pltpu
from jax.sharding import PartitionSpec as P

NX = 128
NY = 96
NZ = 192
ROW_DEV = 16
PAIRS = 8
GA = 64
ZN, YN, CN, BN = 8, 4, 2, 4
HALF_Y = NY // 2
PENCILS = NY * NZ // GA
G_DEV = 640
TILES = G_DEV // 128
MESH = pl.DeviceIdType.MESH
F32 = jnp.float32
BF16 = jnp.bfloat16


def split_np(table):
    high = table.astype(np.float32).astype(jnp.bfloat16)
    low = (table - high.astype(np.float64)).astype(jnp.bfloat16)
    return high, low


def z_table():
    points = np.arange(NZ)
    angle = 2.0 * np.pi * ((points[:, None] * points[None, :]) % NZ) / NZ
    cosine, sine = np.cos(angle), np.sin(angle)
    table = np.zeros((2, 2, 256, 2, 2, 128))
    for parity in range(2):
        rows = slice(64 * parity, 64 * parity + NZ)
        for part_in in range(2):
            for part_out in range(2):
                values = cosine if part_in == part_out else (sine if part_in else -sine)
                for half in range(2):
                    table[parity, part_in, rows, part_out, half, 0:96] = values[:, 96 * half : 96 * half + 96]
    return table.reshape(2, 512, 512)


def y_table():
    k = np.arange(NY)[:, None]
    table = np.zeros((2, NY, 2, 2, HALF_Y))
    for parity in range(2):
        y = 2 * np.arange(HALF_Y)[None, :] + parity
        angle = 2.0 * np.pi * ((k * y) % NY) / NY
        table[0, :, 0, parity] = np.cos(angle)
        table[0, :, 1, parity] = np.sin(angle)
        table[1, :, 0, parity] = -np.sin(angle)
        table[1, :, 1, parity] = np.cos(angle)
    return table.reshape(2 * NY, 4 * HALF_Y)


def x_table():
    angle = 2.0 * np.pi * np.arange(NX) / NX
    norm = 1.0 / math.sqrt(NX * NY * NZ)
    return np.tile(np.stack([np.cos(angle), np.sin(angle)]) * norm, (4, 1)).astype(np.float32)


def split(value):
    high = value.astype(BF16)
    low = (value - high.astype(F32)).astype(BF16)
    return high, low


def dot(a, b):
    return jnp.dot(a, b, preferred_element_type=F32)


def dot3(a_high, a_low, b_high, b_low):
    return dot(a_high, b_high) + (dot(a_high, b_low) + dot(a_low, b_high))


def coordinates():
    band = lax.axis_index("band")
    ga = lax.axis_index("ga")
    return band, ga // 8, (ga // 2) % 4, ga % 2


def device(band, z, y, c):
    return (band, z * 8 + y * 2 + c)


def greet(partners):
    barrier = pltpu.get_barrier_semaphore()
    for partner in partners:
        pl.semaphore_signal(barrier, inc=1, device_id=partner, device_id_type=MESH)
    return lambda: pl.semaphore_wait(barrier, len(partners))


def send(src, dst, send_sem, recv_sem, partner):
    copy = pltpu.make_async_remote_copy(
        src_ref=src, dst_ref=dst, send_sem=send_sem, recv_sem=recv_sem, device_id=partner, device_id_type=MESH
    )
    copy.start()
    return copy


def density_step(first, step, chosen, pv_ref, pc_ref, dens):
    lanes = pl.ds(pl.multiple_of(step * 384, 384), 384)
    y2 = first + step
    for p in range(PAIRS):
        v, q = chosen[p]
        vr = pv_ref[0, v, :, lanes].astype(F32)
        vi = pv_ref[1, v, :, lanes].astype(F32)
        cr = pc_ref[0, q, :, lanes].astype(F32)
        ci = pc_ref[1, q, :, lanes].astype(F32)
        rows = slice(2 * p, 2 * p + 2)
        dens[y2, rows, 0:384] = vr * cr + vi * ci
        dens[y2, rows, 384:768] = vr * ci - vi * cr


def transform_planes(
    chosen, pv_refs, pc_refs, wzh_ref, wzl_ref, wyh_ref, wyl_ref, dens, zed, spec, wait_psi, wait_tables, after_density
):
    for piece in range(PIECES):
        wait_psi(piece)

        @pl.loop(0, HALF_Y // PIECES // 2)
        def _(step):
            for u in range(2):
                density_step(piece * (HALF_Y // PIECES), step * 2 + u, chosen, pv_refs[piece], pc_refs[piece], dens)

    after_density()
    wait_tables()
    for parity in range(2):
        first = 128 * parity
        both = jnp.concatenate([dens[:, :, first : first + 256], dens[:, :, 384 + first : 640 + first]], axis=2)
        high, low = split(both.reshape(768, 512))
        result = dot3(high, low, wzh_ref[parity], wzl_ref[parity])
        for tile in range(4):
            zed[parity, tile] = result[:, 128 * tile : 128 * tile + 128]
    for p in range(PAIRS):
        for plane in range(2):
            row = 2 * p + plane
            halves = [
                jnp.concatenate(
                    [
                        zed[parity, 2 * part + tile, pl.ds(row, HALF_Y, stride=16), :]
                        for part in range(2)
                        for parity in range(2)
                    ],
                    axis=0,
                )
                for tile in range(2)
            ]
            high, low = split(jnp.concatenate(halves, axis=1))
            result = dot3(wyh_ref[...], wyl_ref[...], high, low)
            for part in range(2):
                for tile in range(2):
                    spec[tile, pl.ds(part * 16 + plane * 8 + p, NY, stride=32), :] = result[
                        part * NY : (part + 1) * NY, 128 * tile : 128 * tile + 128
                    ]


def take(table, index):
    return jnp.take_along_axis(table, index, axis=1)


PICK = 384


def partial_block(m, cd, tiles, miller_of, table, plane_of_row, scale, spec, store):
    base = pl.multiple_of(m * 96, 96)
    line = miller_of(0, slice(0, G_DEV))
    second = line >= 96
    third = line >= 192
    sources = []
    for tile in range(3):
        k_row, half = (3 * cd + tile) // 2, (3 * cd + tile) % 2
        sources.append(spec[half, pl.ds(pl.multiple_of(base + 32 * k_row, 32), 32), :])
    if tiles[-1] * 128 >= PICK:
        key = line[:, PICK:] + jnp.where(third[:, PICK:], 64, jnp.where(second[:, PICK:], 32, 0))
        wide = G_DEV - PICK
        ones = jnp.where(
            lax.broadcasted_iota(jnp.int32, (384, wide), 0) == jnp.broadcast_to(key, (384, wide)), 1.0, 0.0
        ).astype(BF16)
        high, low = split(jnp.concatenate(sources, axis=1))
        picked = dot(jnp.concatenate([high, low], axis=0), ones)
        picked = picked[0:32] + picked[32:64]
    for g in tiles:
        lanes = slice(128 * g, 128 * g + 128)
        h = jnp.broadcast_to(miller_of(1, lanes), (8, 128))
        phases = take(table, (h * plane_of_row) & 127)
        c0, s0, c1, s1 = [jnp.broadcast_to(phases[i : i + 1], (8, 128)) for i in range(4)]
        got = []
        if 128 * g < PICK:
            in_second = jnp.broadcast_to(line[:, lanes], (8, 128)) >= 96
            in_third = jnp.broadcast_to(line[:, lanes], (8, 128)) >= 192
            index = jnp.broadcast_to(line[:, lanes], (8, 128)) - jnp.where(in_third, 192, jnp.where(in_second, 96, 0))
            for group in range(4):
                values = [take(source[8 * group : 8 * group + 8], index) for source in sources]
                got.append(jnp.where(in_third, values[2], jnp.where(in_second, values[1], values[0])))
        else:
            columns = slice(128 * g - PICK, 128 * g - PICK + 128)
            got = [picked[8 * group : 8 * group + 8, columns] for group in range(4)]
        re0, re1, im0, im1 = got
        out_re = (c0 * re0 + s0 * im0) + (c1 * re1 + s1 * im1)
        out_im = (c0 * im0 - s0 * re0) + (c1 * im1 - s1 * re1)
        store(slice(0, 8), lanes, out_re * scale)
        store(slice(8, 16), lanes, out_im * scale)


ROWS_AT = (2, 5, 9)
LAGS = (0, 2), (2, 0), (2, 2), (3, 2)
PIECES = 6
CHUNKS = 4
SLOTS = ZN // CHUNKS
FIRST = 3
OWN = ZN - FIRST


def main_kernel(
    pair_ref,
    val_ref,
    cond_ref,
    pv_hbm,
    pc_hbm,
    wzh_hbm,
    wzl_hbm,
    wyh_hbm,
    wyl_hbm,
    wx_ref,
    miller_ref,
    amps_ref,
    rows_ref,
    pv_refs,
    pc_refs,
    wzh_ref,
    wzl_ref,
    wyh_ref,
    wyl_ref,
    dens,
    zed,
    spec,
    lines,
    sums,
    from_core,
    relayed,
    near,
    far,
    total,
    by_z,
    amps,
    rows,
    x_out,
    x_in,
    z_out,
    z_in,
    load_sem,
    send_sem,
    recv_sem,
):
    band, z, y, c = coordinates()
    z_partners = [device(band, (z + d) % ZN, y, c) for d in range(1, ZN)]
    x_partners = [device((band + d) % BN, z, y, c) for d in range(1, BN)]
    core_partner = device(band, z, y, 1 - c)
    plane_partners = [core_partner] + [
        device(band, z, (y + d) % YN, (c + e) % CN) for d in range(1, YN) for e in range(CN)
    ]
    wait_for_partners = greet(z_partners + x_partners + plane_partners)
    psi_loads = []
    for piece in range(PIECES):
        lanes = pl.ds(piece * (NY * NZ // PIECES), NY * NZ // PIECES)
        for n, (src, dst) in enumerate(((pv_hbm, pv_refs[piece]), (pc_hbm, pc_refs[piece]))):
            copy = pltpu.make_async_copy(src.at[:, :, :, lanes], dst, load_sem.at[2 * piece + n])
            copy.start()
            psi_loads.append(copy)
    table_loads = []
    for n, (src, dst) in enumerate(
        ((wzh_hbm, wzh_ref), (wzl_hbm, wzl_ref), (wyh_hbm, wyh_ref), (wyl_hbm, wyl_ref))
    ):
        copy = pltpu.make_async_copy(src, dst, load_sem.at[2 * PIECES + n])
        copy.start()
        table_loads.append(copy)

    def wait_psi(piece):
        for copy in psi_loads[2 * piece : 2 * piece + 2]:
            copy.wait()

    def wait_tables():
        for copy in table_loads:
            copy.wait()

    ahead = (y + 1 + 2 * c) % YN
    behind = (y + 3 - 2 * c) % YN
    across = (y + 2) % YN
    to_ahead = device(band, z, ahead, c)
    to_behind = device(band, z, behind, c)

    k = miller_ref[1:2, :]
    l = miller_ref[2:3, :]
    lines[z, y, c, 0:1, :] = jnp.where(k < 0, k + NY, k) * NZ + jnp.where(l < 0, l + NZ, l) - (z * 8 + y * 2 + c) * PENCILS
    lines[z, y, c, 1:2, :] = miller_ref[0:1, :] & (NX - 1)
    wait_for_partners()

    sent = []

    def start(slot, src, dst, partner):
        copy = send(src, dst, send_sem.at[slot], recv_sem.at[slot], partner)
        sent.append(copy)
        return copy

    mine = lines.at[z, y, c]
    line_copies = [start(n, mine, mine, partner) for n, partner in enumerate(z_partners)]

    def pass_lines_on():
        for copy in line_copies:
            copy.wait_recv()
        block = lines.at[:, y, c]
        for n, partner in enumerate(plane_partners):
            line_copies.append(start(7 + n, block, block, partner))

    chosen = [(pair_ref[0, p] & 1, pair_ref[1, p] & 31) for p in range(PAIRS)]
    pair_rows = lax.broadcasted_iota(jnp.int32, (8, 128), 0)
    gap = jnp.ones((8, 128), F32)
    for p, (v, q) in enumerate(chosen):
        gap = jnp.where(pair_rows == p, cond_ref[q] - val_ref[v], gap)
    scale = jnp.sqrt(4.0 / (gap * math.sqrt(32.0)))
    plane_of_row = 2 * (z * 8 + y * 2 + c) + ((pair_rows >> 1) & 1)
    table = wx_ref[...]

    transform_planes(
        chosen, pv_refs, pc_refs, wzh_ref, wzl_ref, wyh_ref, wyl_ref, dens, zed, spec, wait_psi, wait_tables, pass_lines_on
    )
    for copy in line_copies[7:]:
        copy.wait_recv()

    def place(n):
        return jnp.where(n == 0, across, jnp.where(n == 1, ahead, jnp.where(n == 2, behind, y)))

    def part(ref, chunk, *index):
        return ref.at[(*index, pl.ds(chunk * SLOTS, SLOTS), slice(None), pl.ds(128, G_DEV - 128))]

    def early(ref, *index):
        return ref.at[(*index, slice(None), slice(None), pl.ds(0, 128))]

    def remote(slot, src, dst, partner):
        return pltpu.make_async_remote_copy(
            src_ref=src,
            dst_ref=dst,
            send_sem=send_sem.at[slot],
            recv_sem=recv_sem.at[slot],
            device_id=partner,
            device_id_type=MESH,
        )

    def core_copy(n, chunk):
        yd = place(n)
        return remote(14 + 7 * chunk + n, part(sums, chunk, 1 - c, yd), part(from_core, chunk, yd), core_partner)

    def relay_copy(chunk):
        return remote(14 + 7 * chunk + 4, part(from_core, chunk, across), part(relayed, chunk), to_ahead)

    def back_copy(chunk):
        return remote(14 + 7 * chunk + 5, part(from_core, chunk, behind), part(near, chunk), to_behind)

    def forth_copy(chunk):
        return remote(14 + 7 * chunk + 6, part(from_core, chunk, ahead), part(far, chunk), to_ahead)

    along_z = 14 + 7 * CHUNKS

    def z_copy(slot):
        return remote(
            along_z + slot, total.at[slot], by_z.at[slot], device(band, (z + slot + FIRST) % ZN, y, c)
        )

    def join(n, chunk, yd):
        core_copy(n, chunk).wait_recv()
        part(from_core, chunk, yd)[...] += part(sums, chunk, c, yd)[...]

    def send_relay(chunk):
        join(0, chunk, across)
        relay_copy(chunk).start()

    def send_back(chunk):
        join(1, chunk, behind)
        back_copy(chunk).start()

    def send_forth(chunk):
        join(2, chunk, ahead)
        relay_copy(chunk).wait_recv()
        part(from_core, chunk, ahead)[...] += part(relayed, chunk)[...]
        forth_copy(chunk).start()

    def send_z(chunk):
        core_copy(3, chunk).wait_recv()
        part(total, chunk)[...] = part(from_core, chunk, y)[...] + part(sums, chunk, c, y)[...]
        back_copy(chunk).wait_recv()
        forth_copy(chunk).wait_recv()
        part(total, chunk)[...] += part(near, chunk)[...] + part(far, chunk)[...]
        for i in range(SLOTS):
            slot = chunk * SLOTS + i

            @pl.when(slot != OWN)
            def _():
                z_copy(slot).start()

    steps = 4 * CHUNKS
    actions = [(n * CHUNKS + lag, action) for (n, lag), action in zip(LAGS, (send_relay, send_back, send_forth, send_z))]

    def add_up(n, slots, tiles):
        yd = place(n)
        for slot in slots:
            zd = (z + slot + FIRST) % ZN
            for cd in range(CN):

                def miller_of(kind, lanes):
                    return lines[zd, yd, cd, kind : kind + 1, lanes]

                def store(sublanes, lanes, value):
                    sums[cd, yd, slot, sublanes, lanes] = value

                partial_block(zd * YN + yd, cd, tiles, miller_of, table, plane_of_row, scale, spec, store)

    x_rows = along_z + 8
    z_rows = x_rows + 3
    plane_rows = z_rows + 7
    along_x = plane_rows + 7
    early_at = along_x + 3

    def early_core(n):
        yd = place(n)
        return remote(early_at + n, early(sums, 1 - c, yd), early(from_core, yd), core_partner)

    def early_join(n, yd):
        early_core(n).wait_recv()
        early(from_core, yd)[...] += early(sums, c, yd)[...]

    early_relay = remote(early_at + 4, early(from_core, across), early(relayed), to_ahead)
    early_back = remote(early_at + 5, early(from_core, behind), early(near), to_behind)
    early_forth = remote(early_at + 6, early(from_core, ahead), early(far), to_ahead)

    @pl.loop(0, 4)
    def _(n):
        @pl.loop(0, 2)
        def _(half):
            add_up(n, [half * 4 + i for i in range(4)], [0])

        early_core(n).start()

    early_join(0, across)
    early_relay.start()
    early_join(1, behind)
    early_back.start()

    def own_rows(to_band, z2):
        return total[(2 * to_band + z2 - z - FIRST + 2 * ZN) % ZN, :, 0:128]

    x_row_copies = [remote(x_rows + n, x_out.at[n], x_in.at[band], partner) for n, partner in enumerate(x_partners)]
    z_row_copies = [remote(z_rows + n, z_out, z_in.at[n], partner) for n, partner in enumerate(z_partners)]

    def rows_y():
        early_join(2, ahead)
        early_relay.wait_recv()
        early(from_core, ahead)[...] += early(relayed)[...]
        early_forth.start()

    def rows_x():
        early_core(3).wait_recv()
        early_back.wait_recv()
        early_forth.wait_recv()
        early(total)[...] = (early(from_core, y)[...] + early(sums, c, y)[...]) + (early(near)[...] + early(far)[...])
        for n in range(BN - 1):
            for z2 in range(2):
                x_out[n, z2] = own_rows((band + n + 1) % BN, z2)
            x_row_copies[n].start()
        for z2 in range(2):
            x_in[band, z2] = own_rows(band, z2)

    def rows_z():
        for copy in x_row_copies:
            copy.wait_recv()
        for z2 in range(2):
            parts = [x_in[b, z2] for b in range(BN)]
            for_real = [-piece for piece in parts]
            for_imag = [piece for both in parts for piece in (-both[8:16], both[0:8])]
            z_out[z2] = jnp.concatenate(for_real + for_imag, axis=0).T[0:ROW_DEV]
        for copy in z_row_copies:
            copy.start()

    @pl.loop(0, steps)
    def _(step):
        n = step // CHUNKS
        chunk = step % CHUNKS
        add_up(n, [chunk * SLOTS + i for i in range(SLOTS)], [1, 2, 3, 4])
        core_copy(n, chunk).start()
        for at, action in zip(ROWS_AT, (rows_y, rows_x, rows_z)):
            pl.when(step == at)(action)
        for first, action in actions:

            @pl.when((step >= first) & (step < first + CHUNKS))
            def _():
                action(step - first)

    for step in range(steps, steps + 2 * CHUNKS):
        for first, action in actions:
            if first <= step < first + CHUNKS:
                action(step - first)

    own = z_out[...]
    for n, copy in enumerate(z_row_copies):
        copy.wait_recv()
        own = own + z_in[n]
    for z2 in range(2):
        rows[z2, y, c] = own[z2]
    block = rows.at[:, y, c]
    row_copies = [start(plane_rows + n, block, block, partner) for n, partner in enumerate(plane_partners)]
    result = total[OWN]
    for slot in range(ZN):
        if slot != OWN:
            z_copy(slot).wait_recv()
            result = result + by_z[slot]
    amps[band] = result
    amp_copies = [
        start(along_x + n, amps.at[band], amps.at[band], partner) for n, partner in enumerate(x_partners)
    ]
    for copy in amp_copies:
        copy.wait_recv()
    amps_ref[...] = amps[...]
    for copy in row_copies:
        copy.wait_recv()
    rows_ref[...] = rows[...]
    for copy in sent:
        copy.wait_send()
    for chunk in range(CHUNKS):
        for copy in [core_copy(n, chunk) for n in range(4)] + [relay_copy(chunk), back_copy(chunk), forth_copy(chunk)]:
            copy.wait_send()
    for slot in range(ZN):
        if slot != OWN:
            z_copy(slot).wait_send()
    for copy in [early_core(n) for n in range(4)] + [early_relay, early_back, early_forth] + x_row_copies + z_row_copies:
        copy.wait_send()


def amplitudes(pair_list, val_energy, cond_energy, psi_valence, psi_conduction, miller):
    vmem = pl.BlockSpec(memory_space=pltpu.VMEM)
    smem = pl.BlockSpec(memory_space=pltpu.SMEM)
    wzh, wzl = split_np(z_table())
    wyh, wyl = split_np(y_table())
    tables = [jnp.asarray(t) for t in (wzh, wzl, wyh, wyl, x_table())]
    block = (ZN, 16, G_DEV)
    return pl.pallas_call(
        main_kernel,
        out_shape=(
            jax.ShapeDtypeStruct((BN, 16, G_DEV), F32),
            jax.ShapeDtypeStruct((2, YN, CN, ROW_DEV, 128), F32),
        ),
        in_specs=[smem] * 3 + [pl.BlockSpec(memory_space=pl.ANY)] * 6 + [vmem] * 2,
        out_specs=(vmem, vmem),
        scratch_shapes=[
            [pltpu.VMEM((2, 2, 2, NY * NZ // PIECES), BF16)] * PIECES,
            [pltpu.VMEM((2, 32, 2, NY * NZ // PIECES), BF16)] * PIECES,
            pltpu.VMEM(wzh.shape, BF16),
            pltpu.VMEM(wzl.shape, BF16),
            pltpu.VMEM(wyh.shape, BF16),
            pltpu.VMEM(wyl.shape, BF16),
            pltpu.VMEM((HALF_Y, 16, 768), F32),
            pltpu.VMEM((2, 4, 768, 128), F32),
            pltpu.VMEM((2, NY * 32, 128), F32),
            pltpu.VMEM((ZN, YN, CN, 2, G_DEV), jnp.int32),
            pltpu.VMEM((CN, YN) + block, F32),
            pltpu.VMEM((YN,) + block, F32),
            pltpu.VMEM(block, F32),
            pltpu.VMEM(block, F32),
            pltpu.VMEM(block, F32),
            pltpu.VMEM(block, F32),
            pltpu.VMEM(block, F32),
            pltpu.VMEM((BN, 16, G_DEV), F32),
            pltpu.VMEM((2, YN, CN, ROW_DEV, 128), F32),
            pltpu.VMEM((BN - 1, 2, 16, 128), F32),
            pltpu.VMEM((BN, 2, 16, 128), F32),
            pltpu.VMEM((2, ROW_DEV, 128), F32),
            pltpu.VMEM((ZN - 1, 2, ROW_DEV, 128), F32),
            pltpu.SemaphoreType.DMA((2 * PIECES + 4,)),
            pltpu.SemaphoreType.DMA((14 + 7 * CHUNKS + 35,)),
            pltpu.SemaphoreType.DMA((14 + 7 * CHUNKS + 35,)),
        ],
        compiler_params=pltpu.CompilerParams(
            collective_id=0, has_side_effects=True, vmem_limit_bytes=56 * 1024 * 1024
        ),
        name="amplitudes",
    )(pair_list, val_energy, cond_energy, psi_valence, psi_conduction, *tables, miller)


def slab_kernel(rows_ref, amps_ref, out_ref):
    right_high, right_low = split(amps_ref[...].reshape(64, G_DEV))
    right = jnp.concatenate([right_high, right_low, right_high], axis=0)
    for part in range(2):
        left_high, left_low = split(rows_ref[...].reshape(256, 128)[:, 64 * part : 64 * part + 64])
        out_ref[:, part, :] = dot(jnp.concatenate([left_high, left_high, left_low], axis=1), right)


def slab(rows, amps):
    vmem = pl.BlockSpec(memory_space=pltpu.VMEM)
    return pl.pallas_call(
        slab_kernel,
        out_shape=jax.ShapeDtypeStruct((256, 2, G_DEV), F32),
        in_specs=[vmem, vmem],
        out_specs=vmem,
        compiler_params=pltpu.CompilerParams(vmem_limit_bytes=60 * 1024 * 1024),
        name="slab",
    )(rows, amps)


def per_device(psi_valence, psi_conduction, val_energy, cond_energy, miller, pair_list):
    amps, rows = amplitudes(pair_list, val_energy, cond_energy, psi_valence, psi_conduction, miller)
    return slab(rows, amps)


def solution(mesh):
    return jax.shard_map(
        per_device,
        mesh=mesh,
        in_specs=(
            P(None, None, "ga", None),
            P(None, "band", "ga", None),
            P(),
            P("band"),
            P(None, "ga"),
            P(None, "band"),
        ),
        out_specs=P("band", None, "ga"),
        check_vma=False,
    )
```
